32 devices in a mesh: dp: 4 (over y, x), expert: 4 (over z), tensor: 2 (over core).
Axes of the slice: x: 2, y: 2, z: 4, core: 2. Of those that a mesh axis runs over, the one named last changes fastest.
Arguments:
- grad_out: bfloat16 [768, 7168], P(('dp', 'expert')), may hold values from -6 to 6
- gate_prob: bfloat16 [768, 2], P(('dp', 'expert')), may hold values from 0.049804688 to 0.94921875
- expert_ids: int32 [768, 2], P(('dp', 'expert')), may hold values from 0 to 3, as said below
- slot_positions: int32 [768, 2], P(('dp', 'expert')), may hold values from 0 to 38, as said below
- expert_down: bfloat16 [4, 2496, 7168], P('expert', 'tensor'), may hold values from -0.03125 to 0.03125
- dense_down: bfloat16 [2496, 7168], P(('expert', 'tensor')), may hold values from -0.03125 to 0.03125
- expert_gate_pre: bfloat16 [4, 624, 2496], P('expert', 'dp', 'tensor'), may hold values from -6 to 6
- expert_up_pre: bfloat16 [4, 624, 2496], P('expert', 'dp', 'tensor'), may hold values from -6 to 6
- dense_gate_pre: bfloat16 [768, 2496], P('dp', ('expert', 'tensor')), may hold values from -6 to 6
- dense_up_pre: bfloat16 [768, 2496], P('dp', ('expert', 'tensor')), may hold values from -6 to 6
Outputs:
- expert_gate_grad: bfloat16 [4, 624, 2496], P('expert', 'dp', 'tensor')
- expert_up_grad: bfloat16 [4, 624, 2496], P('expert', 'dp', 'tensor')
- slot_prob_grad: float32 [4, 624], P('expert', 'dp')
- expert_down_grad: bfloat16 [4, 7168, 2496], P('expert', 'dp', 'tensor')
- dense_gate_grad: bfloat16 [768, 2496], P('dp', ('expert', 'tensor'))
- dense_up_grad: bfloat16 [768, 2496], P('dp', ('expert', 'tensor'))
- dense_down_grad: bfloat16 [7168, 2496], P('dp', ('expert', 'tensor'))
The draws below stay inside these ranges and needn't reach their ends.
Inputs may be any that keep to these rules, and one draw needn't show every extreme that they name: `expert_ids`: the two experts of a token differ. In each block of 48 tokens of one index of dp and expert, no expert is named more than 39 times, and one expert is named exactly 39 times; it is the same expert in all 4 blocks of one dp index. `slot_positions`: the rank of an assignment among the assignments of its block of 48 tokens to the same expert, counting tokens in order and a token's first expert before its second.
All inputs are finite; a program needn't handle non-finite values.
Results may differ from the reference program's by a relative error of at most 0.024.
Values may be sent and summed in bfloat16 or wider, within the bound.
A program may use at most 128 MiB of HBM per device.

```python
import jax
import jax.numpy as jnp
from jax import lax

D = 7168
HE = 2496
HD = 2496
TOK_DEV = 48
CAP = 39
EXPERTS = 4
SLOTS = 624
TOKENS = 768
N_DP = 4
N_EXPERT = 4


def routing_table(base_key):
    blocks = N_DP * N_EXPERT
    key_hot, key_perm, key_rot, key_first, key_second = jax.random.split(base_key, 5)
    hot_group = jax.random.randint(key_hot, (N_DP,), 0, N_EXPERT)
    hot_block = jnp.repeat(hot_group, N_EXPERT)[:, None]
    perm_keys = jax.random.split(key_perm, blocks)
    orders = jax.vmap(lambda one_key: jax.random.permutation(one_key, TOK_DEV))(perm_keys)
    ranks = jnp.argsort(orders, axis=1, stable=True).astype(jnp.int32)
    spread = N_EXPERT - 1
    rotation = jax.random.randint(key_rot, (blocks, 1), 0, spread)
    first_off = jax.random.randint(key_first, (blocks, TOK_DEV), 0, spread)
    second_off = jax.random.randint(key_second, (blocks, TOK_DEV), 0, spread - 1)
    hot_rank = ranks < CAP
    offset_one = jnp.where(hot_rank, 0, 1 + first_off)
    offset_two = jnp.where(hot_rank, 1 + (ranks + rotation) % spread, 1 + (first_off + 1 + second_off) % spread)
    chosen = jnp.stack([(hot_block + offset_one) % N_EXPERT, (hot_block + offset_two) % N_EXPERT], axis=-1).astype(jnp.int32)
    flat = chosen.reshape(blocks, 2 * TOK_DEV)
    onehot = (flat[:, :, None] == jnp.arange(N_EXPERT, dtype=jnp.int32)[None, None, :]).astype(jnp.int32)
    before = jnp.cumsum(onehot, axis=1) - onehot
    slots = jnp.sum(before * onehot, axis=-1).astype(jnp.int32)
    return (chosen.reshape(TOKENS, 2), slots.reshape(TOKENS, 2))


def draw_expert_ids(key, part):
    chosen, slots = routing_table(key)
    return chosen


def draw_slot_positions(key, part):
    chosen, slots = routing_table(key)
    return slots


def with_spikes(values, own_key, source, target, parts, factor):
    owner, partner = [(jnp.arange(values.shape[dim]) // (values.shape[dim] // parts)).reshape([-1 if axis == dim else 1 for axis in range(values.ndim)]) for dim in (source, target)]
    chosen = jax.random.permutation(own_key, parts)[partner]
    strong = (owner == chosen) | (owner == (partner + parts // 2) % parts)
    return jnp.where(strong, factor * values, values)


def steps_of(rng, dims, cuts, smallest, largest):
    level = 1.0
    for axis_at, shards_of in cuts:
        heights = jax.random.uniform(jax.random.fold_in(jax.random.fold_in(rng, 6), axis_at), (shards_of,), jnp.float32, smallest / len(cuts), largest / len(cuts))
        level = level * jnp.repeat(jnp.exp(heights), dims[axis_at] // shards_of).reshape((-1,) + (1,) * (len(dims) - 1 - axis_at))
    return level


def centred(own_key, extent, scale, bound, shards=(), kind=jnp.bfloat16):
    gain = steps_of(own_key, extent, shards, -0.22, 0.18) if shards else 1.0
    result = jax.random.normal(own_key, extent, jnp.float32) * scale * gain
    return jnp.minimum(jnp.maximum(result, -bound), bound).astype(kind)


def bell_draw_with(rng, dims, deviation, reach, cuts, heavy, kind=jnp.bfloat16):
    drawn = deviation * jax.random.normal(rng, dims, jnp.float32)
    if cuts:
        drawn = drawn * steps_of(rng, dims, cuts, -0.22, 0.18)
    return jnp.clip(with_spikes(drawn, jax.random.fold_in(rng, 3), *heavy), -reach, reach).astype(kind)


def setup_inputs(seed: int = 0) -> dict:
    seeds = jax.random.split(jax.random.key(seed), 11)
    return {
        "grad_out": bell_draw_with(seeds[0], (TOKENS, D), 1.0, 6.0, ((0, 16),), (0, 1, 16, 2.0)),
        "gate_prob": jnp.clip(0.049804688 + 0.89941406 * jax.random.uniform(seeds[1], (TOKENS, 2), jnp.float32) ** steps_of(seeds[1], (TOKENS, 2), ((0, 16),), -0.2, 0.2), 0.049804688, 0.94921875).astype(jnp.bfloat16),
        "expert_ids": draw_expert_ids(jax.random.fold_in(seeds[10], 71), 0),
        "slot_positions": draw_slot_positions(jax.random.fold_in(seeds[10], 71), 0),
        "expert_down": centred(seeds[4], (EXPERTS, HE, D), (4 * D) ** -0.5, 0.03125, ((0, 4), (1, 2))),
        "dense_down": centred(seeds[5], (HD, D), (4 * D) ** -0.5, 0.03125, ((0, 8),)),
        "expert_gate_pre": centred(seeds[6], (EXPERTS, SLOTS, HE), 1.5, 6.0, ((0, 4), (1, 4), (2, 2))),
        "expert_up_pre": centred(seeds[7], (EXPERTS, SLOTS, HE), 1.0, 6.0, ((0, 4), (1, 4), (2, 2))),
        "dense_gate_pre": centred(seeds[8], (TOKENS, HD), 1.5, 6.0, ((0, 4), (1, 8))),
        "dense_up_pre": centred(seeds[9], (TOKENS, HD), 1.0, 6.0, ((0, 4), (1, 8))),
    }


def silu_parts(gate_val):
    gate_sig = jax.nn.sigmoid(gate_val)
    activated = gate_val * gate_sig
    slope = gate_sig * (1.0 + gate_val * (1.0 - gate_sig))
    return activated, slope


def replica_sum(rows_in, weighted):
    rows_split = rows_in.reshape(N_DP, -1, rows_in.shape[1])
    weighted_split = weighted.reshape(N_DP, -1, weighted.shape[1])

    def add_term(summed, pair):
        term = jnp.dot(pair[0].T, pair[1], preferred_element_type=jnp.float32)
        rounded = lax.optimization_barrier(term.astype(jnp.bfloat16))
        return summed + rounded.astype(jnp.float32), None

    start_sum = jnp.zeros((rows_in.shape[1], weighted.shape[1]), jnp.float32)
    summed, _ = lax.scan(add_term, start_sum, (rows_split, weighted_split))
    return (summed / N_DP).astype(jnp.bfloat16)


def reference(grad_out, gate_prob, expert_ids, slot_positions, expert_down, dense_down, expert_gate_pre, expert_up_pre, dense_gate_pre, dense_up_pre):
    block_index = jnp.arange(TOKENS, dtype=jnp.int32) // TOK_DEV
    row_index = (block_index[:, None] * CAP + slot_positions).astype(jnp.int32)
    routed = jnp.zeros((EXPERTS, SLOTS, D), jnp.bfloat16).at[expert_ids, row_index].set(
        jnp.broadcast_to(grad_out[:, None, :], (TOKENS, 2, D)))
    routed_prob = jnp.zeros((EXPERTS, SLOTS), jnp.float32).at[expert_ids, row_index].set(
        gate_prob.astype(jnp.float32))

    def one_expert(inputs):
        rows_in, prob_in, weight_in, gate_in, up_in = inputs
        back_hidden = jnp.dot(rows_in, weight_in.T, preferred_element_type=jnp.float32)
        gate_val = gate_in.astype(jnp.float32)
        up_val = up_in.astype(jnp.float32)
        activated, slope = silu_parts(gate_val)
        hidden = activated * up_val
        dots = jnp.sum(back_hidden * hidden, axis=1)
        scaled = prob_in[:, None] * back_hidden
        gate_grad = (scaled * up_val * slope).astype(jnp.bfloat16)
        up_grad = (scaled * activated).astype(jnp.bfloat16)
        weighted = (prob_in[:, None] * hidden).astype(jnp.bfloat16)
        down_grad = replica_sum(rows_in, weighted)
        return gate_grad, up_grad, dots, down_grad

    expert_gate_grad, expert_up_grad, slot_prob_grad, expert_down_grad = lax.map(
        one_expert, (routed, routed_prob, expert_down, expert_gate_pre, expert_up_pre))

    back_dense = jnp.dot(grad_out, dense_down.T, preferred_element_type=jnp.float32)
    dense_gate = dense_gate_pre.astype(jnp.float32)
    dense_up = dense_up_pre.astype(jnp.float32)
    dense_act, dense_slope = silu_parts(dense_gate)
    dense_gate_grad = (back_dense * dense_up * dense_slope).astype(jnp.bfloat16)
    dense_up_grad = (back_dense * dense_act).astype(jnp.bfloat16)
    dense_hidden = (dense_act * dense_up).astype(jnp.bfloat16)
    dense_down_grad = replica_sum(grad_out, dense_hidden)
    return (expert_gate_grad, expert_up_grad, slot_prob_grad, expert_down_grad,
            dense_gate_grad, dense_up_grad, dense_down_grad)
```

```python
import functools

import jax
import jax.numpy as jnp
from jax import lax
from jax.experimental import pallas as pl
from jax.experimental.pallas import tpu as pltpu
from jax.sharding import PartitionSpec as P

MESH = pl.DeviceIdType.MESH
BF = jnp.bfloat16
F32 = jnp.float32


def silu_parts(gate_val):
    gate_sig = jax.nn.sigmoid(gate_val)
    activated = gate_val * gate_sig
    slope = gate_sig * (1.0 + gate_val * (1.0 - gate_sig))
    return (activated, slope)


def gather_kernel(
    n_dp, n_z, grad, meta_in, hid_in, dh_in,
    rows, slices, hid, dh, meta,
    loc, z_send, z_recv, sib_send, sl_send, sl_recv, slf_send,
    mz_send, mz_recv, md_send, md_recv, hid_send, hid_recv, dh_send, dh_recv,
):
    d, z, c = lax.axis_index("dp"), lax.axis_index("expert"), lax.axis_index("tensor")
    half = n_dp // 2
    unit = grad.shape[1] // n_dp
    sib = (d, z, 1 - c)

    def remote(src, dst, ssem, rsem, dev):
        return pltpu.make_async_remote_copy(
            src_ref=src, dst_ref=dst, send_sem=ssem, recv_sem=rsem, device_id=dev, device_id_type=MESH
        )

    def when(cond, fn):
        if cond is True:
            fn()
        else:
            pl.when(cond)(fn)

    pending = []

    def launch(cond, make):
        when(cond, lambda: make().start())
        pending.append((cond, make))

    barrier = pltpu.get_barrier_semaphore()

    def greet(dev):
        pl.semaphore_signal(barrier, inc=1, device_id=dev, device_id_type=MESH)

    peers = [lax.rem(d + k, n_dp) for k in range(1, n_dp)]
    greet(sib)
    for q in peers:
        greet((q, z, c))
    pl.when(z > 0)(lambda: greet((d, z - 1, c)))
    pl.when(z < n_z - 1)(lambda: greet((d, z + 1, c)))
    pl.semaphore_wait(barrier, n_dp + jnp.where(z > 0, 1, 0) + jnp.where(z < n_z - 1, 1, 0))

    def cols(j):
        return pl.ds(pl.multiple_of(j * unit, unit), unit)

    def local_copies():
        out = [
            pltpu.make_async_copy(grad.at[:, pl.ds(j * unit, unit)], rows.at[j, z], loc.at[j])
            for j in range(n_dp)
        ]
        out.append(pltpu.make_async_copy(hid_in, hid.at[d], loc.at[n_dp]))
        out.append(pltpu.make_async_copy(dh_in, dh.at[d], loc.at[n_dp + 1]))
        out.append(pltpu.make_async_copy(meta_in, meta.at[d, z], loc.at[n_dp + 2]))
        return out

    def spread(zb, jj, src, ok):
        j = c * half + jj
        launch(ok & (zb <= z) & (z < n_z - 1), lambda: remote(
            src, rows.at[j, zb], z_send.at[0, jj, zb], z_recv.at[j, zb], (d, z + 1, c)))
        launch(ok & (zb >= z) & (z > 0), lambda: remote(
            src, rows.at[j, zb], z_send.at[1, jj, zb], z_recv.at[j, zb], (d, z - 1, c)))
        launch(ok & (j != d), lambda: remote(
            src, slices.at[d, zb], sl_send.at[jj, zb], sl_recv.at[d, zb], (j, z, c)))

    def spread_meta(zb, src, ok):
        launch(ok & (zb <= z) & (z < n_z - 1), lambda: remote(
            src, meta.at[d, zb], mz_send.at[0, zb], mz_recv.at[zb], (d, z + 1, c)))
        launch(ok & (zb >= z) & (z > 0), lambda: remote(
            src, meta.at[d, zb], mz_send.at[1, zb], mz_recv.at[zb], (d, z - 1, c)))

    yes = z >= 0
    spread_meta(z, meta_in, yes)
    for jj in range(half):
        spread(z, jj, grad.at[:, cols(c * half + jj)], yes)
    for k, q in enumerate(peers):
        launch(True, lambda k=k, q=q: remote(
            hid_in, hid.at[d], hid_send.at[k], hid_recv.at[d], (q, z, c)))
        launch(True, lambda k=k, q=q: remote(
            dh_in, dh.at[d], dh_send.at[k], dh_recv.at[d], (q, z, c)))
    for copy in local_copies():
        copy.start()

    def arrived(dst, rsem):
        return remote(dst, dst, loc.at[0], rsem, sib)

    order = [(z + sign * dist, dist) for dist in range(1, n_z) for sign in (-1, 1)]
    for zb, _ in order:
        ok = (zb >= 0) & (zb < n_z)
        pl.when(ok)(lambda: arrived(meta.at[d, zb], mz_recv.at[zb]).wait_recv())
        spread_meta(zb, meta.at[d, zb], ok)
        for jj in range(half):
            j = c * half + jj
            pl.when(ok)(lambda: arrived(rows.at[j, zb], z_recv.at[j, zb]).wait_recv())
            spread(zb, jj, rows.at[j, zb], ok)
            launch(ok, lambda zb=zb, jj=jj, j=j: remote(
                rows.at[j, zb], rows.at[j, zb], sib_send.at[jj, zb], z_recv.at[j, zb], sib))
    copies = local_copies()
    for copy in copies:
        copy.wait()
    for k, q in enumerate(peers):
        launch(True, lambda k=k, q=q: remote(
            meta.at[d], meta.at[d], md_send.at[k], md_recv.at[d], (q, z, c)))
    for zb, _ in order:
        ok = (zb >= 0) & (zb < n_z)
        for jj in range(half):
            j = (1 - c) * half + jj
            pl.when(ok)(lambda: arrived(rows.at[j, zb], z_recv.at[j, zb]).wait_recv())
    own = pltpu.make_async_copy(rows.at[d], slices.at[d], loc.at[0])
    own.start()
    own_half = c == d // half
    for zb, dist in [(z, 0)] + order:
        ok = (zb >= 0) & (zb < n_z)
        for q in peers:
            pl.when(ok)(lambda: arrived(slices.at[q, zb], sl_recv.at[q, zb]).wait_recv())
            launch(ok & own_half, lambda zb=zb, q=q: remote(
                slices.at[q, zb], slices.at[q, zb], slf_send.at[q, zb], sl_recv.at[q, zb], sib))
    for q in peers:
        arrived(hid.at[q], hid_recv.at[q]).wait_recv()
        arrived(dh.at[q], dh_recv.at[q]).wait_recv()
        arrived(meta.at[q], md_recv.at[q]).wait_recv()
    own.wait()
    for cond, make in pending:
        when(cond, lambda: make().wait_send())


def gather_all(grad_out, meta_in, hid_in, dh_in, n_dp, n_z):
    tok, width = grad_out.shape
    unit = width // n_dp
    half = n_dp // 2
    vm = pl.BlockSpec(memory_space=pltpu.VMEM)
    hbm = pl.BlockSpec(memory_space=pl.ANY)
    dma = pltpu.SemaphoreType.DMA
    return pl.pallas_call(
        functools.partial(gather_kernel, n_dp, n_z),
        out_shape=(
            jax.ShapeDtypeStruct((n_dp, n_z, tok, unit), BF),
            jax.ShapeDtypeStruct((n_dp, n_z, tok, unit), BF),
            jax.ShapeDtypeStruct((n_dp,) + hid_in.shape, BF),
            jax.ShapeDtypeStruct((n_dp,) + dh_in.shape, BF),
            jax.ShapeDtypeStruct((n_dp, n_z) + meta_in.shape, BF),
        ),
        in_specs=[hbm, vm, vm, vm],
        out_specs=(vm,) * 5,
        scratch_shapes=[
            dma((n_dp + 3,)),
            dma((2, half, n_z)), dma((n_dp, n_z)), dma((half, n_z)),
            dma((half, n_z)), dma((n_dp, n_z)), dma((n_dp, n_z)),
            dma((2, n_z)), dma((n_z,)), dma((n_dp,)), dma((n_dp,)),
            dma((n_dp,)), dma((n_dp,)), dma((n_dp,)), dma((n_dp,)),
        ],
        compiler_params=pltpu.CompilerParams(
            collective_id=0, has_side_effects=True, vmem_limit_bytes=48 * 2**20
        ),
    )(grad_out, meta_in, hid_in, dh_in)


def local_fast(
    grad_out, gate_prob, expert_ids, slot_positions, expert_down, dense_down,
    expert_gate_pre, expert_up_pre, dense_gate_pre, dense_up_pre,
):
    n_z = lax.axis_size("expert")
    n_dp = lax.axis_size("dp")
    me = lax.axis_index("expert")
    tok, width = grad_out.shape
    unit = width // n_dp
    slots = expert_gate_pre.shape[1]
    capacity = slots // n_z
    padded = -(-slots // 16) * 16
    meta_in = jnp.concatenate(
        [expert_ids.astype(BF), slot_positions.astype(BF), gate_prob, jnp.zeros((tok, 122), BF)], axis=1
    )
    gate_val = expert_gate_pre[0].astype(F32)
    up_val = expert_up_pre[0].astype(F32)
    activated, slope = silu_parts(gate_val)
    hidden = activated * up_val
    dense_gate = dense_gate_pre.astype(F32)
    dense_up = dense_up_pre.astype(F32)
    dense_act, dense_slope = silu_parts(dense_gate)
    hid_in = jnp.pad(hidden.astype(BF), ((0, padded - slots), (0, 0)))
    dh_in = (dense_act * dense_up).astype(BF)

    rows, slices, hid, dh, meta = gather_all(grad_out, meta_in, hid_in, dh_in, n_dp, n_z)

    info = meta.reshape(n_dp, n_z * tok, 128).astype(F32)
    block = (jnp.arange(n_z * tok) // tok * capacity).astype(F32)[None, :, None]
    span = jnp.arange(padded).astype(F32)[None, None, :]
    mine = me.astype(F32)
    first = (info[:, :, 0:1] == mine) & (info[:, :, 2:3] + block == span)
    second = (info[:, :, 1:2] == mine) & (info[:, :, 3:4] + block == span)
    weight = jnp.where(first, info[:, :, 4:5], 0.0) + jnp.where(second, info[:, :, 5:6], 0.0)
    here = lax.axis_index("dp")
    pick = (first | second).astype(BF)
    pick_d = lax.dynamic_index_in_dim(pick, here, 0, keepdims=False)
    slot_prob = jnp.sum(lax.dynamic_index_in_dim(weight, here, 0, keepdims=False), axis=0)[:slots]

    rows_tok = rows.reshape(n_dp, n_z * tok, unit)
    routed = jnp.einsum("ts,jtu->sju", pick_d[:, :slots], rows_tok, preferred_element_type=BF)
    back_hidden = lax.dot_general(
        routed.reshape(slots, width), expert_down[0], (((1,), (1,)), ((), ())), preferred_element_type=F32
    )
    slot_dots = lax.psum(jnp.sum(back_hidden * hidden, axis=1), "tensor")
    scaled = slot_prob[:, None] * back_hidden
    expert_gate_grad = (scaled * up_val * slope).astype(BF)[None]
    expert_up_grad = (scaled * activated).astype(BF)[None]
    back_dense = jnp.einsum(
        "jtu,hju->th", rows_tok, dense_down.reshape(-1, n_dp, unit), preferred_element_type=F32
    )
    dense_gate_grad = (back_dense * dense_up * dense_slope).astype(BF)
    dense_up_grad = (back_dense * dense_act).astype(BF)

    weighted = jnp.einsum("qts,qsh->qth", weight.astype(BF), hid, preferred_element_type=F32).astype(BF)
    every = slices.reshape(-1, unit)
    contract = (((0,), (0,)), ((), ()))
    expert_sum = lax.dot_general(
        every, weighted.reshape(every.shape[0], -1), contract, preferred_element_type=F32
    )
    dense_sum = lax.dot_general(
        every, dh.reshape(every.shape[0], -1), contract, preferred_element_type=F32
    )
    return (
        expert_gate_grad,
        expert_up_grad,
        slot_dots[None],
        (expert_sum / n_dp).astype(BF)[None],
        dense_gate_grad,
        dense_up_grad,
        (dense_sum / n_dp).astype(BF),
    )


def local_plain(
    grad_out,
    gate_prob,
    expert_ids,
    slot_positions,
    expert_down,
    dense_down,
    expert_gate_pre,
    expert_up_pre,
    dense_gate_pre,
    dense_up_pre,
):
    n_expert = lax.axis_size("expert")
    n_replica = lax.axis_size("dp")
    width = grad_out.shape[1]
    capacity = expert_gate_pre.shape[1] // n_expert
    flat_ids = expert_ids.reshape(-1)
    flat_slots = slot_positions.reshape(-1)
    repeated = jnp.repeat(grad_out, 2, axis=0)
    send_rows = (
        jnp.zeros((n_expert, capacity, width), jnp.bfloat16).at[flat_ids, flat_slots].set(repeated)
    )
    send_prob = (
        jnp.zeros((n_expert, capacity), jnp.bfloat16)
        .at[flat_ids, flat_slots]
        .set(gate_prob.reshape(-1))
    )
    recv_rows, recv_prob = (
        lax.all_to_all(send_rows, "expert", split_axis=0, concat_axis=0, tiled=True),
        lax.all_to_all(send_prob, "expert", split_axis=0, concat_axis=0, tiled=True),
    )
    slot_rows = recv_rows.reshape(n_expert * capacity, width)
    slot_prob = recv_prob.reshape(-1).astype(jnp.float32)
    weight_local = expert_down[0]
    back_hidden = lax.dot_general(
        slot_rows, weight_local, (((1,), (1,)), ((), ())), preferred_element_type=jnp.float32
    )
    gate_val = expert_gate_pre[0].astype(jnp.float32)
    up_val = expert_up_pre[0].astype(jnp.float32)
    activated, slope = silu_parts(gate_val)
    hidden = activated * up_val
    partial_dots = jnp.sum(back_hidden * hidden, axis=1)
    slot_dots = lax.psum(partial_dots, "tensor")
    scaled = slot_prob[:, None] * back_hidden
    expert_gate_grad = (scaled * up_val * slope).astype(jnp.bfloat16)[None]
    expert_up_grad = (scaled * activated).astype(jnp.bfloat16)[None]
    weighted = (slot_prob[:, None] * hidden).astype(jnp.bfloat16)
    expert_summed = lax.psum_scatter(
        lax.dot_general(
            slot_rows, weighted, (((0,), (0,)), ((), ())), preferred_element_type=jnp.float32
        ).astype(jnp.bfloat16),
        "dp",
        scatter_dimension=0,
        tiled=True,
    ).astype(jnp.float32)
    expert_down_grad = (expert_summed / n_replica).astype(jnp.bfloat16)[None]
    shard_rows = lax.all_gather(grad_out, "expert", axis=0, tiled=True)
    back_dense = lax.dot_general(
        shard_rows, dense_down, (((1,), (1,)), ((), ())), preferred_element_type=jnp.float32
    )
    dense_gate = dense_gate_pre.astype(jnp.float32)
    dense_up = dense_up_pre.astype(jnp.float32)
    dense_act, dense_slope = silu_parts(dense_gate)
    gate_buffer = (back_dense * dense_up * dense_slope).astype(jnp.bfloat16)
    up_buffer = (back_dense * dense_act).astype(jnp.bfloat16)
    dense_hidden = (dense_act * dense_up).astype(jnp.bfloat16)
    weight_sum = lax.dot_general(
        shard_rows, dense_hidden, (((0,), (0,)), ((), ())), preferred_element_type=jnp.float32
    )
    dense_summed = lax.psum_scatter(
        weight_sum.astype(jnp.bfloat16), "dp", scatter_dimension=0, tiled=True
    ).astype(jnp.float32)
    dense_down_grad = (dense_summed / n_replica).astype(jnp.bfloat16)
    return (
        expert_gate_grad,
        expert_up_grad,
        slot_dots[None],
        expert_down_grad,
        gate_buffer,
        up_buffer,
        dense_down_grad,
    )


def solution(mesh):
    sizes = mesh.shape
    fits = sizes["tensor"] == 2 and sizes["dp"] == 4

    def local(*args):
        aligned = args[0].shape[1] % (sizes["dp"] * 128) == 0 and args[0].shape[0] % 16 == 0
        return (local_fast if fits and aligned else local_plain)(*args)

    return jax.shard_map(
        local,
        mesh=mesh,
        in_specs=(
            P(("dp", "expert"), None),
            P(("dp", "expert"), None),
            P(("dp", "expert"), None),
            P(("dp", "expert"), None),
            P("expert", "tensor", None),
            P(("expert", "tensor"), None),
            P("expert", "dp", "tensor"),
            P("expert", "dp", "tensor"),
            P("dp", ("expert", "tensor")),
            P("dp", ("expert", "tensor")),
        ),
        out_specs=(
            P("expert", "dp", "tensor"),
            P("expert", "dp", "tensor"),
            P("expert", "dp"),
            P("expert", "dp", "tensor"),
            P("dp", ("expert", "tensor")),
            P("dp", ("expert", "tensor")),
            P("dp", ("expert", "tensor")),
        ),
        check_vma=False,
    )
```

```python
import functools

import jax
import jax.numpy as jnp
from jax import lax
from jax.experimental import pallas as pl
from jax.experimental.pallas import tpu as pltpu
from jax.sharding import PartitionSpec as P

MESH = pl.DeviceIdType.MESH
BF = jnp.bfloat16
F32 = jnp.float32


def silu_parts(gate_val):
    gate_sig = jax.nn.sigmoid(gate_val)
    activated = gate_val * gate_sig
    slope = gate_sig * (1.0 + gate_val * (1.0 - gate_sig))
    return (activated, slope)


def selection(info, mine, capacity, slots, tok):
    info = info.astype(F32)
    tokens = info.shape[0]
    block = lax.broadcasted_iota(jnp.int32, (tokens, slots), 0) // tok
    span = (lax.broadcasted_iota(jnp.int32, (tokens, slots), 1) - block * capacity).astype(F32)
    first = (info[:, 0:1] == mine) & (info[:, 2:3] == span)
    second = (info[:, 1:2] == mine) & (info[:, 3:4] == span)
    weight = jnp.where(first, info[:, 4:5], 0.0) + jnp.where(second, info[:, 5:6], 0.0)
    pick = jnp.where(first | second, 1.0, 0.0)
    return pick.astype(BF), weight.astype(BF)


def layer_kernel(
    n_dp, n_z, grad, meta_in, expert_w, dense_w, gate_pre, up_pre, dense_gate_pre, dense_up_pre,
    slices, weighted, dh, gate_out, up_out, dgate_out, dup_out, dots_out,
    rows, hid, meta, w, dw, acc, dacc, dots,
    loc, w_sem, dw_sem, z_send, z_recv, sib_send, sl_send, sl_recv, slf_send,
    mz_send, mz_recv, md_send, md_recv, hid_send, hid_recv, dh_send, dh_recv,
    hf_send, hf_recv, df_send, df_recv, dot_send, dot_recv,
):
    d, z, c = lax.axis_index("dp"), lax.axis_index("expert"), lax.axis_index("tensor")
    half = n_dp // 2
    tok = grad.shape[0]
    unit = grad.shape[1] // n_dp
    slots = gate_pre.shape[1]
    padded = hid.shape[1]
    capacity = slots // n_z
    sib = (d, z, 1 - c)
    flip_x = d + 1 - 2 * lax.rem(d, 2)
    flip_y = lax.rem(d + 2, n_dp)
    diag = lax.rem(flip_x + 2, n_dp)
    peers = [flip_x, flip_y, diag]

    def remote(src, dst, ssem, rsem, dev):
        return pltpu.make_async_remote_copy(
            src_ref=src, dst_ref=dst, send_sem=ssem, recv_sem=rsem, device_id=dev, device_id_type=MESH
        )

    def when(cond, fn):
        if cond is True:
            fn()
        else:
            pl.when(cond)(fn)

    pending = []

    def launch(cond, make):
        when(cond, lambda: make().start())
        pending.append((cond, make))

    barrier = pltpu.get_barrier_semaphore()

    def greet(dev):
        pl.semaphore_signal(barrier, inc=1, device_id=dev, device_id_type=MESH)

    greet(sib)
    for q in peers:
        greet((q, z, c))
    pl.when(z > 0)(lambda: greet((d, z - 1, c)))
    pl.when(z < n_z - 1)(lambda: greet((d, z + 1, c)))

    def cols(j):
        return pl.ds(pl.multiple_of(j * unit, unit), unit)

    def local_copies():
        out = [
            pltpu.make_async_copy(grad.at[:, pl.ds(j * unit, unit)], rows.at[j, z], loc.at[j])
            for j in range(n_dp)
        ]
        out.append(pltpu.make_async_copy(meta_in, meta.at[d, z], loc.at[n_dp]))
        return out

    def weight_copies(j):
        return (
            pltpu.make_async_copy(expert_w.at[0, :, cols(j)], w.at[j], w_sem.at[j]),
            pltpu.make_async_copy(dense_w.at[:, cols(j)], dw.at[j], dw_sem.at[j]),
        )

    for copy in local_copies():
        copy.start()

    hid[d] = jnp.zeros(hid.shape[1:], BF)
    activated, _ = silu_parts(gate_pre[0].astype(F32))
    hid[d, pl.ds(0, slots), :] = (activated * up_pre[0].astype(F32)).astype(BF)
    activated, _ = silu_parts(dense_gate_pre[...].astype(F32))
    dh[d] = (activated * dense_up_pre[...].astype(F32)).astype(BF)

    pl.semaphore_wait(barrier, n_dp + jnp.where(z > 0, 1, 0) + jnp.where(z < n_z - 1, 1, 0))

    def spread(zb, jj, src, ok):
        j = c * half + jj
        launch(ok & (zb <= z) & (z < n_z - 1), lambda: remote(
            src, rows.at[j, zb], z_send.at[0, jj, zb], z_recv.at[j, zb], (d, z + 1, c)))
        launch(ok & (zb >= z) & (z > 0), lambda: remote(
            src, rows.at[j, zb], z_send.at[1, jj, zb], z_recv.at[j, zb], (d, z - 1, c)))
        launch(ok & (j != d), lambda: remote(
            src, slices.at[d, zb], sl_send.at[jj, zb], sl_recv.at[d, zb], (j, z, c)))

    def spread_meta(zb, src, ok):
        launch(ok & (zb <= z) & (z < n_z - 1), lambda: remote(
            src, meta.at[d, zb], mz_send.at[0, zb], mz_recv.at[zb], (d, z + 1, c)))
        launch(ok & (zb >= z) & (z > 0), lambda: remote(
            src, meta.at[d, zb], mz_send.at[1, zb], mz_recv.at[zb], (d, z - 1, c)))

    yes = z >= 0
    spread_meta(z, meta_in, yes)
    for jj in range(half):
        spread(z, jj, grad.at[:, cols(c * half + jj)], yes)
    for k, q in enumerate(peers[:2]):
        launch(True, lambda k=k, q=q: remote(
            hid.at[d], hid.at[d], hid_send.at[k], hid_recv.at[d], (q, z, c)))
        launch(True, lambda k=k, q=q: remote(
            dh.at[d], dh.at[d], dh_send.at[k], dh_recv.at[d], (q, z, c)))
    for j in range(n_dp):
        for copy in weight_copies(j):
            copy.start()

    def arrived(dst, rsem):
        return remote(dst, dst, loc.at[0], rsem, sib)

    def pass_hidden():
        for k, (source, target) in enumerate(((flip_x, flip_y), (flip_y, flip_x))):
            arrived(hid.at[source], hid_recv.at[source]).wait_recv()
            arrived(dh.at[source], dh_recv.at[source]).wait_recv()
            part = pl.ds(k * (padded // 2), padded // 2)
            dpart = pl.ds(k * (dh.shape[1] // 2), dh.shape[1] // 2)
            launch(True, lambda k=k, source=source, target=target, part=part: remote(
                hid.at[source, part], hid.at[source, part], hf_send.at[k], hf_recv.at[k], (target, z, c)))
            launch(True, lambda k=k, source=source, target=target, dpart=dpart: remote(
                dh.at[source, dpart], dh.at[source, dpart], df_send.at[k], df_recv.at[k], (target, z, c)))

    own_half = c == d // half

    def pass_slices(zb, ok):
        for q in peers:
            pl.when(ok)(lambda: arrived(slices.at[q, zb], sl_recv.at[q, zb]).wait_recv())
            launch(ok & own_half, lambda q=q: remote(
                slices.at[q, zb], slices.at[q, zb], slf_send.at[q, zb], sl_recv.at[q, zb], sib))

    order = [(z + sign * dist, dist) for dist in range(1, n_z) for sign in (-1, 1)]
    for step, (zb, dist) in enumerate(order):
        if step == 2 * (n_z - 2):
            pass_hidden()
        ok = (zb >= 0) & (zb < n_z)
        pl.when(ok)(lambda: arrived(meta.at[d, zb], mz_recv.at[zb]).wait_recv())
        spread_meta(zb, meta.at[d, zb], ok)
        for jj in range(half):
            j = c * half + jj
            pl.when(ok)(lambda: arrived(rows.at[j, zb], z_recv.at[j, zb]).wait_recv())
            spread(zb, jj, rows.at[j, zb], ok)
            launch(ok, lambda zb=zb, jj=jj, j=j: remote(
                rows.at[j, zb], rows.at[j, zb], sib_send.at[jj, zb], z_recv.at[j, zb], sib))
    for copy in local_copies():
        copy.wait()
    for k, q in enumerate(peers):
        launch(True, lambda k=k, q=q: remote(
            meta.at[d], meta.at[d], md_send.at[k], md_recv.at[d], (q, z, c)))
    pass_slices(z, yes)
    for zb, dist in order[:2]:
        pass_slices(zb, (zb >= 0) & (zb < n_z))
    for zb, _ in order:
        ok = (zb >= 0) & (zb < n_z)
        for jj in range(half):
            j = (1 - c) * half + jj
            pl.when(ok)(lambda: arrived(rows.at[j, zb], z_recv.at[j, zb]).wait_recv())
    own = pltpu.make_async_copy(rows.at[d], slices.at[d], loc.at[0])
    own.start()

    mine = z.astype(F32)
    info = meta[d].reshape(n_z * tok, meta.shape[-1])
    pick, weight = selection(info, mine, capacity, padded, tok)
    by_token = (((0,), (0,)), ((), ()))
    by_width = (((1,), (1,)), ((), ()))
    acc[...] = jnp.zeros_like(acc)
    dacc[...] = jnp.zeros_like(dacc)

    def back(j, _):
        for copy in weight_copies(j):
            copy.wait()
        tokens = rows[j].reshape(n_z * tok, unit)
        routed = lax.dot_general(pick, tokens, by_token, preferred_element_type=F32).astype(BF)
        acc[...] += lax.dot_general(routed, w[j], by_width, preferred_element_type=F32)
        dacc[...] += lax.dot_general(tokens, dw[j], by_width, preferred_element_type=F32)
        return 0

    lax.fori_loop(0, n_dp, back, 0)

    prob = lax.dot_general(
        weight, jnp.ones((n_z * tok, 128), BF), by_token, preferred_element_type=F32
    )[:slots, 0:1]
    back_hidden = acc[pl.ds(0, slots), :]
    up_val = up_pre[0].astype(F32)
    activated, slope = silu_parts(gate_pre[0].astype(F32))
    partial = jnp.sum(back_hidden * (activated * up_val), axis=1, keepdims=True)
    dots[0] = jnp.zeros(dots.shape[1:], F32)
    dots[0, pl.ds(0, slots), :] = jnp.broadcast_to(partial, (slots, 128))
    launch(True, lambda: remote(dots.at[0], dots.at[1], dot_send, dot_recv, sib))
    for zb, dist in order[2:]:
        pass_slices(zb, (zb >= 0) & (zb < n_z))
    scaled = prob * back_hidden
    gate_out[0] = (scaled * up_val * slope).astype(BF)
    up_out[0] = (scaled * activated).astype(BF)
    dense_up = dense_up_pre[...].astype(F32)
    activated, slope = silu_parts(dense_gate_pre[...].astype(F32))
    dgate_out[...] = (dacc[...] * dense_up * slope).astype(BF)
    dup_out[...] = (dacc[...] * activated).astype(BF)

    for q in peers:
        arrived(meta.at[q], md_recv.at[q]).wait_recv()
    for k in range(2):
        part = pl.ds(k * (padded // 2), padded // 2)
        dpart = pl.ds(k * (dh.shape[1] // 2), dh.shape[1] // 2)
        arrived(hid.at[diag, part], hf_recv.at[k]).wait_recv()
        arrived(dh.at[diag, dpart], df_recv.at[k]).wait_recv()

    def place(q, _):
        _, weight_q = selection(
            meta[q].reshape(n_z * tok, meta.shape[-1]), mine, capacity, padded, tok
        )
        weighted[q] = jnp.dot(weight_q, hid[q], preferred_element_type=F32).astype(BF)
        return 0

    lax.fori_loop(0, n_dp, place, 0)
    arrived(dots.at[1], dot_recv).wait_recv()
    dots_out[...] = dots[0] + dots[1]
    own.wait()
    for cond, make in pending:
        when(cond, lambda: make().wait_send())


def layer(grad_out, meta_in, expert_down, dense_down, gate_pre, up_pre, dense_gate, dense_up, n_dp, n_z):
    tok, width = grad_out.shape
    unit = width // n_dp
    half = n_dp // 2
    _, slots, he = gate_pre.shape
    tokens, hd = dense_gate.shape
    padded = -(-slots // 32) * 32
    vm = pl.BlockSpec(memory_space=pltpu.VMEM)
    hbm = pl.BlockSpec(memory_space=pl.ANY)
    dma = pltpu.SemaphoreType.DMA
    shape = jax.ShapeDtypeStruct
    return pl.pallas_call(
        functools.partial(layer_kernel, n_dp, n_z),
        out_shape=(
            shape((n_dp, n_z, tok, unit), BF),
            shape((n_dp, tokens, he), BF),
            shape((n_dp, tokens, hd), BF),
            shape(gate_pre.shape, BF),
            shape(gate_pre.shape, BF),
            shape(dense_gate.shape, BF),
            shape(dense_gate.shape, BF),
            shape((padded, 128), F32),
        ),
        in_specs=[hbm, vm, hbm, hbm, vm, vm, vm, vm],
        out_specs=(vm,) * 8,
        scratch_shapes=[
            pltpu.VMEM((n_dp, n_z, tok, unit), BF),
            pltpu.VMEM((n_dp, padded, he), BF),
            pltpu.VMEM((n_dp, n_z) + meta_in.shape, BF),
            pltpu.VMEM((n_dp, he, unit), BF),
            pltpu.VMEM((n_dp, hd, unit), BF),
            pltpu.VMEM((padded, he), F32),
            pltpu.VMEM((tokens, hd), F32),
            pltpu.VMEM((2, padded, 128), F32),
            dma((n_dp + 1,)), dma((n_dp,)), dma((n_dp,)),
            dma((2, half, n_z)), dma((n_dp, n_z)), dma((half, n_z)),
            dma((half, n_z)), dma((n_dp, n_z)), dma((n_dp, n_z)),
            dma((2, n_z)), dma((n_z,)), dma((n_dp,)), dma((n_dp,)),
            dma((2,)), dma((n_dp,)), dma((2,)), dma((n_dp,)),
            dma((2,)), dma((2,)), dma((2,)), dma((2,)), dma, dma,
        ],
        compiler_params=pltpu.CompilerParams(
            collective_id=0, has_side_effects=True, vmem_limit_bytes=58 * 2**20
        ),
    )(grad_out, meta_in, expert_down, dense_down, gate_pre, up_pre, dense_gate, dense_up)


def local_fast(
    grad_out, gate_prob, expert_ids, slot_positions, expert_down, dense_down,
    expert_gate_pre, expert_up_pre, dense_gate_pre, dense_up_pre,
):
    n_z = lax.axis_size("expert")
    n_dp = lax.axis_size("dp")
    tok = grad_out.shape[0]
    slots = expert_gate_pre.shape[1]
    meta_in = jnp.concatenate(
        [expert_ids.astype(BF), slot_positions.astype(BF), gate_prob, jnp.zeros((tok, 122), BF)], axis=1
    )
    slices, weighted, dh, gate_grad, up_grad, dgate_grad, dup_grad, dots = layer(
        grad_out, meta_in, expert_down, dense_down,
        expert_gate_pre, expert_up_pre, dense_gate_pre, dense_up_pre, n_dp, n_z,
    )
    every = slices.reshape(-1, slices.shape[-1])
    contract = (((0,), (0,)), ((), ()))
    expert_sum = lax.dot_general(
        every, weighted.reshape(every.shape[0], -1), contract, preferred_element_type=F32
    )
    dense_sum = lax.dot_general(
        every, dh.reshape(every.shape[0], -1), contract, preferred_element_type=F32
    )
    return (
        gate_grad,
        up_grad,
        dots[:slots, 0][None],
        (expert_sum / n_dp).astype(BF)[None],
        dgate_grad,
        dup_grad,
        (dense_sum / n_dp).astype(BF),
    )


def local_plain(
    grad_out,
    gate_prob,
    expert_ids,
    slot_positions,
    expert_down,
    dense_down,
    expert_gate_pre,
    expert_up_pre,
    dense_gate_pre,
    dense_up_pre,
):
    n_expert = lax.axis_size("expert")
    n_replica = lax.axis_size("dp")
    width = grad_out.shape[1]
    capacity = expert_gate_pre.shape[1] // n_expert
    flat_ids = expert_ids.reshape(-1)
    flat_slots = slot_positions.reshape(-1)
    repeated = jnp.repeat(grad_out, 2, axis=0)
    send_rows = (
        jnp.zeros((n_expert, capacity, width), jnp.bfloat16).at[flat_ids, flat_slots].set(repeated)
    )
    send_prob = (
        jnp.zeros((n_expert, capacity), jnp.bfloat16)
        .at[flat_ids, flat_slots]
        .set(gate_prob.reshape(-1))
    )
    recv_rows, recv_prob = (
        lax.all_to_all(send_rows, "expert", split_axis=0, concat_axis=0, tiled=True),
        lax.all_to_all(send_prob, "expert", split_axis=0, concat_axis=0, tiled=True),
    )
    slot_rows = recv_rows.reshape(n_expert * capacity, width)
    slot_prob = recv_prob.reshape(-1).astype(jnp.float32)
    weight_local = expert_down[0]
    back_hidden = lax.dot_general(
        slot_rows, weight_local, (((1,), (1,)), ((), ())), preferred_element_type=jnp.float32
    )
    gate_val = expert_gate_pre[0].astype(jnp.float32)
    up_val = expert_up_pre[0].astype(jnp.float32)
    activated, slope = silu_parts(gate_val)
    hidden = activated * up_val
    partial_dots = jnp.sum(back_hidden * hidden, axis=1)
    slot_dots = lax.psum(partial_dots, "tensor")
    scaled = slot_prob[:, None] * back_hidden
    expert_gate_grad = (scaled * up_val * slope).astype(jnp.bfloat16)[None]
    expert_up_grad = (scaled * activated).astype(jnp.bfloat16)[None]
    weighted = (slot_prob[:, None] * hidden).astype(jnp.bfloat16)
    expert_summed = lax.psum_scatter(
        lax.dot_general(
            slot_rows, weighted, (((0,), (0,)), ((), ())), preferred_element_type=jnp.float32
        ).astype(jnp.bfloat16),
        "dp",
        scatter_dimension=0,
        tiled=True,
    ).astype(jnp.float32)
    expert_down_grad = (expert_summed / n_replica).astype(jnp.bfloat16)[None]
    shard_rows = lax.all_gather(grad_out, "expert", axis=0, tiled=True)
    back_dense = lax.dot_general(
        shard_rows, dense_down, (((1,), (1,)), ((), ())), preferred_element_type=jnp.float32
    )
    dense_gate = dense_gate_pre.astype(jnp.float32)
    dense_up = dense_up_pre.astype(jnp.float32)
    dense_act, dense_slope = silu_parts(dense_gate)
    gate_buffer = (back_dense * dense_up * dense_slope).astype(jnp.bfloat16)
    up_buffer = (back_dense * dense_act).astype(jnp.bfloat16)
    dense_hidden = (dense_act * dense_up).astype(jnp.bfloat16)
    weight_sum = lax.dot_general(
        shard_rows, dense_hidden, (((0,), (0,)), ((), ())), preferred_element_type=jnp.float32
    )
    dense_summed = lax.psum_scatter(
        weight_sum.astype(jnp.bfloat16), "dp", scatter_dimension=0, tiled=True
    ).astype(jnp.float32)
    dense_down_grad = (dense_summed / n_replica).astype(jnp.bfloat16)
    return (
        expert_gate_grad,
        expert_up_grad,
        slot_dots[None],
        expert_down_grad,
        gate_buffer,
        up_buffer,
        dense_down_grad,
    )


def solution(mesh):
    sizes = mesh.shape
    fits = sizes["tensor"] == 2 and sizes["dp"] == 4

    def local(*args):
        aligned = args[0].shape[1] % (sizes["dp"] * 128) == 0 and args[0].shape[0] % 16 == 0
        return (local_fast if fits and aligned else local_plain)(*args)

    return jax.shard_map(
        local,
        mesh=mesh,
        in_specs=(
            P(("dp", "expert"), None),
            P(("dp", "expert"), None),
            P(("dp", "expert"), None),
            P(("dp", "expert"), None),
            P("expert", "tensor", None),
            P(("expert", "tensor"), None),
            P("expert", "dp", "tensor"),
            P("expert", "dp", "tensor"),
            P("dp", ("expert", "tensor")),
            P("dp", ("expert", "tensor")),
        ),
        out_specs=(
            P("expert", "dp", "tensor"),
            P("expert", "dp", "tensor"),
            P("expert", "dp"),
            P("expert", "dp", "tensor"),
            P("dp", ("expert", "tensor")),
            P("dp", ("expert", "tensor")),
            P("dp", ("expert", "tensor")),
        ),
        check_vma=False,
    )
```

```python
import functools

import jax
import jax.numpy as jnp
from jax import lax
from jax.experimental import pallas as pl
from jax.experimental.pallas import tpu as pltpu
from jax.sharding import PartitionSpec as P

MESH = pl.DeviceIdType.MESH
BF = jnp.bfloat16
F32 = jnp.float32
VMEM_LIMIT = 52 * 2**20


def silu_parts(gate_val):
    gate_sig = jax.nn.sigmoid(gate_val)
    activated = gate_val * gate_sig
    slope = gate_sig * (1.0 + gate_val * (1.0 - gate_sig))
    return (activated, slope)


def selection(info, mine, capacity, slots, tok):
    info = info.astype(F32)
    tokens = info.shape[0]
    block = lax.broadcasted_iota(jnp.int32, (tokens, slots), 0) // tok
    span = (lax.broadcasted_iota(jnp.int32, (tokens, slots), 1) - block * capacity).astype(F32)
    first = (info[:, 0:1] == mine) & (info[:, 2:3] == span)
    second = (info[:, 1:2] == mine) & (info[:, 3:4] == span)
    weight = jnp.where(first, info[:, 4:5], 0.0) + jnp.where(second, info[:, 5:6], 0.0)
    pick = jnp.where(first | second, 1.0, 0.0)
    return pick.astype(BF), weight.astype(BF)


def layer_kernel(
    n_dp, n_z, grad, ids, places, probs, expert_w, dense_w, gate_pre, up_pre, dense_gate_pre, dense_up_pre,
    slices, weighted, dh, gate_out, up_out, dgate_out, dup_out, dots_out,
    rows, hid, meta, table, w, dw, acc, dacc, dots,
    loc, w_sem, dw_sem, z_send, z_recv, sib_send, sl_send, sl_recv, slf_send,
    mz_send, mz_recv, md_send, md_recv, hid_send, hid_recv, dh_send, dh_recv,
    hf_send, hf_recv, df_send, df_recv, dot_send, dot_recv,
):
    d, z, c = lax.axis_index("dp"), lax.axis_index("expert"), lax.axis_index("tensor")
    half = n_dp // 2
    tok = grad.shape[0]
    unit = grad.shape[1] // n_dp
    slots = gate_pre.shape[1]
    padded = hid.shape[1]
    capacity = slots // n_z
    sib = (d, z, 1 - c)
    flip_x = d + 1 - 2 * lax.rem(d, 2)
    flip_y = lax.rem(d + 2, n_dp)
    diag = lax.rem(flip_x + 2, n_dp)
    peers = [flip_x, flip_y, diag]

    def remote(src, dst, ssem, rsem, dev):
        return pltpu.make_async_remote_copy(
            src_ref=src, dst_ref=dst, send_sem=ssem, recv_sem=rsem, device_id=dev, device_id_type=MESH
        )

    def when(cond, fn):
        if cond is True:
            fn()
        else:
            pl.when(cond)(fn)

    pending = []

    def launch(cond, make):
        when(cond, lambda: make().start())
        pending.append((cond, make))

    barrier = pltpu.get_barrier_semaphore()

    def greet(dev):
        pl.semaphore_signal(barrier, inc=1, device_id=dev, device_id_type=MESH)

    greet(sib)
    for q in peers:
        greet((q, z, c))
    pl.when(z > 0)(lambda: greet((d, z - 1, c)))
    pl.when(z < n_z - 1)(lambda: greet((d, z + 1, c)))

    def cols(j):
        return pl.ds(pl.multiple_of(j * unit, unit), unit)

    def local_copies():
        return [
            pltpu.make_async_copy(grad.at[:, pl.ds(j * unit, unit)], rows.at[j, z], loc.at[j])
            for j in range(n_dp)
        ]

    def weight_copies(j):
        return (
            pltpu.make_async_copy(expert_w.at[0, :, cols(j)], w.at[j], w_sem.at[j]),
            pltpu.make_async_copy(dense_w.at[:, cols(j)], dw.at[j], dw_sem.at[j]),
        )

    for copy in local_copies():
        copy.start()
    for j in range(n_dp):
        for copy in weight_copies((j * half) % n_dp + (j * half) // n_dp):
            copy.start()

    table[...] = jnp.zeros(table.shape, F32)
    for k, ref in enumerate((ids, places, probs)):
        table[pl.ds(2 * k, 2), pl.ds(0, tok)] = ref[...].astype(F32)
    meta[d, z] = table[...].T[:tok].astype(BF)
    hid[d] = jnp.zeros(hid.shape[1:], BF)
    activated, _ = silu_parts(gate_pre[0].astype(F32))
    hid[d, pl.ds(0, slots), :] = (activated * up_pre[0].astype(F32)).astype(BF)
    activated, _ = silu_parts(dense_gate_pre[...].astype(F32))
    dh[d] = (activated * dense_up_pre[...].astype(F32)).astype(BF)

    pl.semaphore_wait(barrier, n_dp + jnp.where(z > 0, 1, 0) + jnp.where(z < n_z - 1, 1, 0))

    def along_z(zb, jj, src, ok):
        j = c * half + jj
        launch(ok & (zb <= z) & (z < n_z - 1), lambda: remote(
            src, rows.at[j, zb], z_send.at[0, jj, zb], z_recv.at[j, zb], (d, z + 1, c)))
        launch(ok & (zb >= z) & (z > 0), lambda: remote(
            src, rows.at[j, zb], z_send.at[1, jj, zb], z_recv.at[j, zb], (d, z - 1, c)))

    def over_dp(zb, jj, src, ok):
        j = c * half + jj
        launch(ok & (j != d), lambda: remote(
            src, slices.at[d, zb], sl_send.at[jj, zb], sl_recv.at[d, zb], (j, z, c)))

    def spread_meta(zb, ok):
        src = meta.at[d, zb]
        launch(ok & (zb <= z) & (z < n_z - 1), lambda: remote(
            src, src, mz_send.at[0, zb], mz_recv.at[zb], (d, z + 1, c)))
        launch(ok & (zb >= z) & (z > 0), lambda: remote(
            src, src, mz_send.at[1, zb], mz_recv.at[zb], (d, z - 1, c)))

    yes = z >= 0
    spread_meta(z, yes)
    along_z(z, 0, grad.at[:, cols(c * half)], yes)
    for jj in range(half):
        over_dp(z, jj, grad.at[:, cols(c * half + jj)], yes)
    for k, q in enumerate(peers[:2]):
        launch(True, lambda k=k, q=q: remote(
            hid.at[d], hid.at[d], hid_send.at[k], hid_recv.at[d], (q, z, c)))
        launch(True, lambda k=k, q=q: remote(
            dh.at[d], dh.at[d], dh_send.at[k], dh_recv.at[d], (q, z, c)))

    def arrived(dst, rsem):
        return remote(dst, dst, loc.at[0], rsem, sib)

    def pass_hidden():
        for k, (source, target) in enumerate(((flip_x, flip_y), (flip_y, flip_x))):
            arrived(hid.at[source], hid_recv.at[source]).wait_recv()
            arrived(dh.at[source], dh_recv.at[source]).wait_recv()
            part = pl.ds(k * (padded // 2), padded // 2)
            dpart = pl.ds(k * (dh.shape[1] // 2), dh.shape[1] // 2)
            launch(True, lambda k=k, source=source, target=target, part=part: remote(
                hid.at[source, part], hid.at[source, part], hf_send.at[k], hf_recv.at[k], (target, z, c)))
            launch(True, lambda k=k, source=source, target=target, dpart=dpart: remote(
                dh.at[source, dpart], dh.at[source, dpart], df_send.at[k], df_recv.at[k], (target, z, c)))

    own_half = c == d // half

    def pass_slices(zb, ok):
        for q in peers:
            pl.when(ok)(lambda: arrived(slices.at[q, zb], sl_recv.at[q, zb]).wait_recv())
            launch(ok & own_half, lambda q=q: remote(
                slices.at[q, zb], slices.at[q, zb], slf_send.at[q, zb], sl_recv.at[q, zb], sib))

    def ring(dist):
        return [(zb, (zb >= 0) & (zb < n_z)) for zb in (z - dist, z + dist)]

    def relay_rows(jj, dist):
        j = c * half + jj
        for zb, ok in ring(dist):
            pl.when(ok)(lambda: arrived(rows.at[j, zb], z_recv.at[j, zb]).wait_recv())
            along_z(zb, jj, rows.at[j, zb], ok)
            launch(ok, lambda zb=zb: remote(
                rows.at[j, zb], rows.at[j, zb], sib_send.at[jj, zb], z_recv.at[j, zb], sib))
            over_dp(zb, jj, rows.at[j, zb], ok)

    def relay_slices(dist):
        for zb, ok in [(z, yes)] if dist == 0 else ring(dist):
            pass_slices(zb, ok)

    for dist in range(1, n_z):
        for zb, ok in ring(dist):
            pl.when(ok)(lambda: arrived(meta.at[d, zb], mz_recv.at[zb]).wait_recv())
            spread_meta(zb, ok)
    for k, q in enumerate(peers):
        launch(True, lambda k=k, q=q: remote(
            meta.at[d], meta.at[d], md_send.at[k], md_recv.at[d], (q, z, c)))

    mine = z.astype(F32)

    def place(q):
        _, weight_q = selection(
            meta[q].reshape(n_z * tok, meta.shape[-1]), mine, capacity, padded, tok
        )
        weighted[q] = jnp.dot(weight_q, hid[q], preferred_element_type=F32).astype(BF)

    acc[...] = jnp.zeros_like(acc)
    dacc[...] = jnp.zeros_like(dacc)
    by_token = (((0,), (0,)), ((), ()))
    by_width = (((1,), (1,)), ((), ()))

    def back(jj):
        info = meta[d].reshape(n_z * tok, meta.shape[-1])
        pick, _ = selection(info, mine, capacity, padded, tok)

        def unit_of(i, _):
            j = jj + half * i
            for copy in weight_copies(j):
                copy.wait()
            tokens = rows[j].reshape(n_z * tok, unit)
            routed = lax.dot_general(pick, tokens, by_token, preferred_element_type=F32).astype(BF)
            acc[...] += lax.dot_general(routed, w[j], by_width, preferred_element_type=F32)
            dacc[...] += lax.dot_general(tokens, dw[j], by_width, preferred_element_type=F32)
            return 0

        lax.fori_loop(0, n_dp // half, unit_of, 0)

    def from_sibling(jj):
        j = (1 - c) * half + jj
        for dist in range(1, n_z):
            for zb, ok in ring(dist):
                pl.when(ok)(lambda: arrived(rows.at[j, zb], z_recv.at[j, zb]).wait_recv())

    for jj in range(half):
        for dist in range(1, n_z):
            if jj == half - 1 and dist == n_z - 1:
                pass_hidden()
                for q in peers:
                    arrived(meta.at[q], md_recv.at[q]).wait_recv()
                place(d)
                place(flip_x)
                place(flip_y)
                for copy in local_copies():
                    copy.wait()
                for early in range(half - 1):
                    from_sibling(early)
                    back(early)
                relay_slices(0)
            relay_rows(jj, dist)
            if dist == 1 and jj < half - 1:
                along_z(z, jj + 1, grad.at[:, cols(c * half + jj + 1)], yes)
    relay_slices(1)
    from_sibling(half - 1)
    own = pltpu.make_async_copy(rows.at[d], slices.at[d], loc.at[0])
    own.start()
    back(half - 1)

    _, weight = selection(meta[d].reshape(n_z * tok, meta.shape[-1]), mine, capacity, padded, tok)
    prob = lax.dot_general(
        weight, jnp.ones((n_z * tok, 128), BF), by_token, preferred_element_type=F32
    )[:slots, 0:1]
    back_hidden = acc[pl.ds(0, slots), :]
    up_val = up_pre[0].astype(F32)
    activated, slope = silu_parts(gate_pre[0].astype(F32))
    partial = jnp.sum(back_hidden * (activated * up_val), axis=1, keepdims=True)
    dots[0] = jnp.zeros(dots.shape[1:], F32)
    dots[0, pl.ds(0, slots), :] = jnp.broadcast_to(partial, (slots, 128))
    launch(True, lambda: remote(dots.at[0], dots.at[1], dot_send, dot_recv, sib))
    for dist in range(2, n_z):
        relay_slices(dist)
    scaled = prob * back_hidden
    gate_out[0] = (scaled * up_val * slope).astype(BF)
    up_out[0] = (scaled * activated).astype(BF)
    dense_up = dense_up_pre[...].astype(F32)
    activated, slope = silu_parts(dense_gate_pre[...].astype(F32))
    dgate_out[...] = (dacc[...] * dense_up * slope).astype(BF)
    dup_out[...] = (dacc[...] * activated).astype(BF)

    for k in range(2):
        part = pl.ds(k * (padded // 2), padded // 2)
        dpart = pl.ds(k * (dh.shape[1] // 2), dh.shape[1] // 2)
        arrived(hid.at[diag, part], hf_recv.at[k]).wait_recv()
        arrived(dh.at[diag, dpart], df_recv.at[k]).wait_recv()
    place(diag)
    arrived(dots.at[1], dot_recv).wait_recv()
    dots_out[...] = (dots[0] + dots[1]).T[0:1, :slots]
    own.wait()
    for cond, make in pending:
        when(cond, lambda: make().wait_send())


def layer(
    grad_out, ids, places, probs, expert_down, dense_down, gate_pre, up_pre, dense_gate, dense_up, n_dp, n_z
):
    tok, width = grad_out.shape
    unit = width // n_dp
    half = n_dp // 2
    _, slots, he = gate_pre.shape
    tokens, hd = dense_gate.shape
    padded = -(-slots // 32) * 32
    square = -(-slots // 128) * 128
    vm = pl.BlockSpec(memory_space=pltpu.VMEM)
    hbm = pl.BlockSpec(memory_space=pl.ANY)
    dma = pltpu.SemaphoreType.DMA
    shape = jax.ShapeDtypeStruct
    return pl.pallas_call(
        functools.partial(layer_kernel, n_dp, n_z),
        out_shape=(
            shape((n_dp, n_z, tok, unit), BF),
            shape((n_dp, tokens, he), BF),
            shape((n_dp, tokens, hd), BF),
            shape(gate_pre.shape, BF),
            shape(gate_pre.shape, BF),
            shape(dense_gate.shape, BF),
            shape(dense_gate.shape, BF),
            shape((1, slots), F32),
        ),
        in_specs=[hbm, vm, vm, vm, hbm, hbm, vm, vm, vm, vm],
        out_specs=(vm,) * 8,
        scratch_shapes=[
            pltpu.VMEM((n_dp, n_z, tok, unit), BF),
            pltpu.VMEM((n_dp, padded, he), BF),
            pltpu.VMEM((n_dp, n_z, tok, 128), BF),
            pltpu.VMEM((128, 128), F32),
            pltpu.VMEM((n_dp, he, unit), BF),
            pltpu.VMEM((n_dp, hd, unit), BF),
            pltpu.VMEM((padded, he), F32),
            pltpu.VMEM((tokens, hd), F32),
            pltpu.VMEM((2, square, 128), F32),
            dma((n_dp + 1,)), dma((n_dp,)), dma((n_dp,)),
            dma((2, half, n_z)), dma((n_dp, n_z)), dma((half, n_z)),
            dma((half, n_z)), dma((n_dp, n_z)), dma((n_dp, n_z)),
            dma((2, n_z)), dma((n_z,)), dma((n_dp,)), dma((n_dp,)),
            dma((2,)), dma((n_dp,)), dma((2,)), dma((n_dp,)),
            dma((2,)), dma((2,)), dma((2,)), dma((2,)), dma, dma,
        ],
        compiler_params=pltpu.CompilerParams(
            collective_id=0, has_side_effects=True, vmem_limit_bytes=VMEM_LIMIT
        ),
    )(grad_out, ids, places, probs, expert_down, dense_down, gate_pre, up_pre, dense_gate, dense_up)


def final_kernel(scale, slices, weighted, dh, *refs):
    count = (len(refs) - 3) // 2
    given, (expert_out, dense_out), taken, sem = (
        refs[:count], refs[count:count + 2], refs[count + 2:-1], refs[-1]
    )
    copies = [pltpu.make_async_copy(a, b, sem.at[i]) for i, (a, b) in enumerate(zip(given, taken))]
    step = pl.program_id(0)

    @pl.when(step == 0)
    def _():
        for copy in copies:
            copy.start()

    contract = (((0,), (0,)), ((), ()))
    right = slices[...]
    expert_out[0] = (
        lax.dot_general(weighted[...], right, contract, preferred_element_type=F32) * scale
    ).astype(BF)
    dense_out[...] = (
        lax.dot_general(dh[...], right, contract, preferred_element_type=F32) * scale
    ).astype(BF)

    @pl.when(step == pl.num_programs(0) - 1)
    def _():
        for copy in copies:
            copy.wait()


def final(slices, weighted, dh, small, scale):
    tokens, unit = slices.shape
    he, hd = weighted.shape[1], dh.shape[1]
    tile = unit // 2 if unit % 256 == 0 else unit
    hbm = pl.BlockSpec(memory_space=pl.ANY)
    shape = jax.ShapeDtypeStruct
    return pl.pallas_call(
        functools.partial(final_kernel, scale),
        grid=(unit // tile,),
        out_shape=(shape((1, he, unit), BF), shape((hd, unit), BF))
        + tuple(shape(a.shape, a.dtype) for a in small),
        in_specs=[
            pl.BlockSpec((tokens, tile), lambda i: (0, i)),
            pl.BlockSpec((tokens, he), lambda i: (0, 0)),
            pl.BlockSpec((tokens, hd), lambda i: (0, 0)),
        ] + [hbm] * len(small),
        out_specs=(
            pl.BlockSpec((1, he, tile), lambda i: (0, 0, i)),
            pl.BlockSpec((hd, tile), lambda i: (0, i)),
        ) + (hbm,) * len(small),
        scratch_shapes=[pltpu.SemaphoreType.DMA((len(small),))],
        compiler_params=pltpu.CompilerParams(vmem_limit_bytes=32 * 2**20),
    )(slices, weighted, dh, *small)


def local_fast(
    grad_out, gate_prob, expert_ids, slot_positions, expert_down, dense_down,
    expert_gate_pre, expert_up_pre, dense_gate_pre, dense_up_pre,
):
    n_z = lax.axis_size("expert")
    n_dp = lax.axis_size("dp")
    slices, weighted, dh, *small = layer(
        grad_out, expert_ids.T, slot_positions.T, gate_prob.T, expert_down, dense_down,
        expert_gate_pre, expert_up_pre, dense_gate_pre, dense_up_pre, n_dp, n_z,
    )
    tokens = slices.shape[0] * slices.shape[1] * slices.shape[2]
    expert_grad, dense_grad, gate_grad, up_grad, dgate_grad, dup_grad, dots = final(
        slices.reshape(tokens, -1), weighted.reshape(tokens, -1), dh.reshape(tokens, -1), small, 1.0 / n_dp
    )
    return (gate_grad, up_grad, dots, expert_grad.transpose(0, 2, 1), dgate_grad, dup_grad, dense_grad.T)


def local_plain(
    grad_out,
    gate_prob,
    expert_ids,
    slot_positions,
    expert_down,
    dense_down,
    expert_gate_pre,
    expert_up_pre,
    dense_gate_pre,
    dense_up_pre,
):
    n_expert = lax.axis_size("expert")
    n_replica = lax.axis_size("dp")
    width = grad_out.shape[1]
    capacity = expert_gate_pre.shape[1] // n_expert
    flat_ids = expert_ids.reshape(-1)
    flat_slots = slot_positions.reshape(-1)
    repeated = jnp.repeat(grad_out, 2, axis=0)
    send_rows = (
        jnp.zeros((n_expert, capacity, width), jnp.bfloat16).at[flat_ids, flat_slots].set(repeated)
    )
    send_prob = (
        jnp.zeros((n_expert, capacity), jnp.bfloat16)
        .at[flat_ids, flat_slots]
        .set(gate_prob.reshape(-1))
    )
    recv_rows, recv_prob = (
        lax.all_to_all(send_rows, "expert", split_axis=0, concat_axis=0, tiled=True),
        lax.all_to_all(send_prob, "expert", split_axis=0, concat_axis=0, tiled=True),
    )
    slot_rows = recv_rows.reshape(n_expert * capacity, width)
    slot_prob = recv_prob.reshape(-1).astype(jnp.float32)
    weight_local = expert_down[0]
    back_hidden = lax.dot_general(
        slot_rows, weight_local, (((1,), (1,)), ((), ())), preferred_element_type=jnp.float32
    )
    gate_val = expert_gate_pre[0].astype(jnp.float32)
    up_val = expert_up_pre[0].astype(jnp.float32)
    activated, slope = silu_parts(gate_val)
    hidden = activated * up_val
    partial_dots = jnp.sum(back_hidden * hidden, axis=1)
    slot_dots = lax.psum(partial_dots, "tensor")
    scaled = slot_prob[:, None] * back_hidden
    expert_gate_grad = (scaled * up_val * slope).astype(jnp.bfloat16)[None]
    expert_up_grad = (scaled * activated).astype(jnp.bfloat16)[None]
    weighted = (slot_prob[:, None] * hidden).astype(jnp.bfloat16)
    expert_summed = lax.psum_scatter(
        lax.dot_general(
            slot_rows, weighted, (((0,), (0,)), ((), ())), preferred_element_type=jnp.float32
        ).astype(jnp.bfloat16),
        "dp",
        scatter_dimension=0,
        tiled=True,
    ).astype(jnp.float32)
    expert_down_grad = (expert_summed / n_replica).astype(jnp.bfloat16)[None]
    shard_rows = lax.all_gather(grad_out, "expert", axis=0, tiled=True)
    back_dense = lax.dot_general(
        shard_rows, dense_down, (((1,), (1,)), ((), ())), preferred_element_type=jnp.float32
    )
    dense_gate = dense_gate_pre.astype(jnp.float32)
    dense_up = dense_up_pre.astype(jnp.float32)
    dense_act, dense_slope = silu_parts(dense_gate)
    gate_buffer = (back_dense * dense_up * dense_slope).astype(jnp.bfloat16)
    up_buffer = (back_dense * dense_act).astype(jnp.bfloat16)
    dense_hidden = (dense_act * dense_up).astype(jnp.bfloat16)
    weight_sum = lax.dot_general(
        shard_rows, dense_hidden, (((0,), (0,)), ((), ())), preferred_element_type=jnp.float32
    )
    dense_summed = lax.psum_scatter(
        weight_sum.astype(jnp.bfloat16), "dp", scatter_dimension=0, tiled=True
    ).astype(jnp.float32)
    dense_down_grad = (dense_summed / n_replica).astype(jnp.bfloat16)
    return (
        expert_gate_grad,
        expert_up_grad,
        slot_dots[None],
        expert_down_grad,
        gate_buffer,
        up_buffer,
        dense_down_grad,
    )


def solution(mesh):
    sizes = mesh.shape
    fits = sizes["tensor"] == 2 and sizes["dp"] == 4

    def local(*args):
        aligned = args[0].shape[1] % (sizes["dp"] * 128) == 0 and args[0].shape[0] % 16 == 0
        return (local_fast if fits and aligned else local_plain)(*args)

    return jax.shard_map(
        local,
        mesh=mesh,
        in_specs=(
            P(("dp", "expert"), None),
            P(("dp", "expert"), None),
            P(("dp", "expert"), None),
            P(("dp", "expert"), None),
            P("expert", "tensor", None),
            P(("expert", "tensor"), None),
            P("expert", "dp", "tensor"),
            P("expert", "dp", "tensor"),
            P("dp", ("expert", "tensor")),
            P("dp", ("expert", "tensor")),
        ),
        out_specs=(
            P("expert", "dp", "tensor"),
            P("expert", "dp", "tensor"),
            P("expert", "dp"),
            P("expert", "dp", "tensor"),
            P("dp", ("expert", "tensor")),
            P("dp", ("expert", "tensor")),
            P("dp", ("expert", "tensor")),
        ),
        check_vma=False,
    )
```

```python
import functools

import jax
import jax.numpy as jnp
from jax import lax
from jax.experimental import pallas as pl
from jax.experimental.pallas import tpu as pltpu
from jax.sharding import PartitionSpec as P

MESH = pl.DeviceIdType.MESH
BF = jnp.bfloat16
F32 = jnp.float32
VMEM_LIMIT = 60 * 2**20


def silu_parts(gate_val):
    gate_sig = jax.nn.sigmoid(gate_val)
    activated = gate_val * gate_sig
    slope = gate_sig * (1.0 + gate_val * (1.0 - gate_sig))
    return (activated, slope)


def selection(info, mine, capacity, slots, tok):
    info = info.astype(F32)
    tokens = info.shape[0]
    block = lax.broadcasted_iota(jnp.int32, (tokens, slots), 0) // tok
    span = (lax.broadcasted_iota(jnp.int32, (tokens, slots), 1) - block * capacity).astype(F32)
    first = (info[:, 0:1] == mine) & (info[:, 2:3] == span)
    second = (info[:, 1:2] == mine) & (info[:, 3:4] == span)
    weight = jnp.where(first, info[:, 4:5], 0.0) + jnp.where(second, info[:, 5:6], 0.0)
    pick = jnp.where(first | second, 1.0, 0.0)
    return pick.astype(BF), weight.astype(BF)


def layer_kernel(
    n_dp, n_z, grad, ids, places, probs, expert_w, dense_w, gate_pre, up_pre, dense_gate_pre, dense_up_pre,
    slices, weighted, dh, gate_out, up_out, dgate_out, dup_out, dots_out,
    rows, hid, meta, table, w, dw, acc, dacc, dots,
    loc, w_sem, dw_sem, z_send, z_recv, sib_send, sl_send, sl_recv, slf_send,
    mz_send, mz_recv, md_send, md_recv, hid_send, hid_recv, dh_send, dh_recv,
    hf_send, hf_recv, df_send, df_recv, dot_send, dot_recv, slz_send,
):
    d, z, c = lax.axis_index("dp"), lax.axis_index("expert"), lax.axis_index("tensor")
    half = n_dp // 2
    tok = grad.shape[0]
    unit = grad.shape[1] // n_dp
    slots = gate_pre.shape[1]
    padded = hid.shape[1]
    capacity = slots // n_z
    sib = (d, z, 1 - c)
    flip_x = d + 1 - 2 * lax.rem(d, 2)
    flip_y = lax.rem(d + 2, n_dp)
    diag = lax.rem(flip_x + 2, n_dp)
    peers = [flip_x, flip_y, diag]

    def remote(src, dst, ssem, rsem, dev):
        return pltpu.make_async_remote_copy(
            src_ref=src, dst_ref=dst, send_sem=ssem, recv_sem=rsem, device_id=dev, device_id_type=MESH
        )

    def when(cond, fn):
        if cond is True:
            fn()
        else:
            pl.when(cond)(fn)

    pending = []

    def launch(cond, make):
        when(cond, lambda: make().start())
        pending.append((cond, make))

    barrier = pltpu.get_barrier_semaphore()

    def greet(dev):
        pl.semaphore_signal(barrier, inc=1, device_id=dev, device_id_type=MESH)

    greet(sib)
    for q in peers:
        greet((q, z, c))
    pl.when(z > 0)(lambda: greet((d, z - 1, c)))
    pl.when(z < n_z - 1)(lambda: greet((d, z + 1, c)))

    def cols(j):
        return pl.ds(pl.multiple_of(j * unit, unit), unit)

    def local_copies():
        return [
            pltpu.make_async_copy(grad.at[:, pl.ds(j * unit, unit)], rows.at[j, z], loc.at[j])
            for j in range(n_dp)
        ]

    def weight_copies(j):
        return (
            pltpu.make_async_copy(expert_w.at[0, :, cols(j)], w.at[j], w_sem.at[j]),
            pltpu.make_async_copy(dense_w.at[:, cols(j)], dw.at[j], dw_sem.at[j]),
        )

    for copy in local_copies():
        copy.start()
    for j in range(n_dp):
        for copy in weight_copies((j * half) % n_dp + (j * half) // n_dp):
            copy.start()

    table[...] = jnp.zeros(table.shape, F32)
    for k, ref in enumerate((ids, places, probs)):
        table[pl.ds(2 * k, 2), pl.ds(0, tok)] = ref[...].astype(F32)
    meta[d, z] = table[...].T[:tok].astype(BF)
    hid[d] = jnp.zeros(hid.shape[1:], BF)
    activated, _ = silu_parts(gate_pre[0].astype(F32))
    hid[d, pl.ds(0, slots), :] = (activated * up_pre[0].astype(F32)).astype(BF)
    activated, _ = silu_parts(dense_gate_pre[...].astype(F32))
    dh[d] = (activated * dense_up_pre[...].astype(F32)).astype(BF)

    pl.semaphore_wait(barrier, n_dp + jnp.where(z > 0, 1, 0) + jnp.where(z < n_z - 1, 1, 0))

    def along_z(zb, jj, src, ok):
        j = c * half + jj
        launch(ok & (zb <= z) & (z < n_z - 1), lambda: remote(
            src, rows.at[j, zb], z_send.at[0, jj, zb], z_recv.at[j, zb], (d, z + 1, c)))
        launch(ok & (zb >= z) & (z > 0), lambda: remote(
            src, rows.at[j, zb], z_send.at[1, jj, zb], z_recv.at[j, zb], (d, z - 1, c)))

    def over_dp(zb, jj, src, ok):
        j = c * half + jj
        launch(ok & (j != d), lambda: remote(
            src, slices.at[d, zb], sl_send.at[jj, zb], sl_recv.at[d, zb], (j, z, c)))

    def spread_meta(zb, ok):
        src = meta.at[d, zb]
        launch(ok & (zb <= z) & (z < n_z - 1), lambda: remote(
            src, src, mz_send.at[0, zb], mz_recv.at[zb], (d, z + 1, c)))
        launch(ok & (zb >= z) & (z > 0), lambda: remote(
            src, src, mz_send.at[1, zb], mz_recv.at[zb], (d, z - 1, c)))

    yes = z >= 0
    spread_meta(z, yes)
    along_z(z, 0, grad.at[:, cols(c * half)], yes)
    for jj in range(half):
        over_dp(z, jj, grad.at[:, cols(c * half + jj)], yes)
    for k, q in enumerate(peers[:2]):
        launch(True, lambda k=k, q=q: remote(
            hid.at[d], hid.at[d], hid_send.at[k], hid_recv.at[d], (q, z, c)))
        launch(True, lambda k=k, q=q: remote(
            dh.at[d], dh.at[d], dh_send.at[k], dh_recv.at[d], (q, z, c)))

    def arrived(dst, rsem):
        return remote(dst, dst, loc.at[0], rsem, sib)

    def pass_hidden():
        for k, (source, target) in enumerate(((flip_x, flip_y), (flip_y, flip_x))):
            arrived(hid.at[source], hid_recv.at[source]).wait_recv()
            arrived(dh.at[source], dh_recv.at[source]).wait_recv()
            part = pl.ds(k * (padded // 2), padded // 2)
            dpart = pl.ds(k * (dh.shape[1] // 2), dh.shape[1] // 2)
            launch(True, lambda k=k, source=source, target=target, part=part: remote(
                hid.at[source, part], hid.at[source, part], hf_send.at[k], hf_recv.at[k], (target, z, c)))
            launch(True, lambda k=k, source=source, target=target, dpart=dpart: remote(
                dh.at[source, dpart], dh.at[source, dpart], df_send.at[k], df_recv.at[k], (target, z, c)))

    own_half = c == d // half

    def pass_slices(zb, ok, own=False):
        for q in peers:
            pl.when(ok)(lambda: arrived(slices.at[q, zb], sl_recv.at[q, zb]).wait_recv())
            launch(ok & own_half, lambda q=q: remote(
                slices.at[q, zb], slices.at[q, zb], slf_send.at[q, zb], sl_recv.at[q, zb], sib))
            for k, (step, there) in enumerate(((1, z < n_z - 1), (-1, z > 0)) if own else ()):
                launch(own_half & there, lambda q=q, k=k, step=step: remote(
                    slices.at[q, zb], slices.at[q, zb], slz_send.at[k, q], sl_recv.at[q, zb],
                    (d, z + step, c)))

    def ring(dist):
        return [(zb, (zb >= 0) & (zb < n_z)) for zb in (z - dist, z + dist)]

    def relay_rows(jj, dist):
        j = c * half + jj
        for zb, ok in ring(dist):
            pl.when(ok)(lambda: arrived(rows.at[j, zb], z_recv.at[j, zb]).wait_recv())
            along_z(zb, jj, rows.at[j, zb], ok)
            launch(ok, lambda zb=zb: remote(
                rows.at[j, zb], rows.at[j, zb], sib_send.at[jj, zb], z_recv.at[j, zb], sib))
            if dist > 1:
                over_dp(zb, jj, rows.at[j, zb], ok)

    def relay_slices(dist):
        for zb, ok in [(z, yes)] if dist == 0 else ring(dist):
            pass_slices(zb, ok, dist == 0)

    for dist in range(1, n_z):
        for zb, ok in ring(dist):
            pl.when(ok)(lambda: arrived(meta.at[d, zb], mz_recv.at[zb]).wait_recv())
            spread_meta(zb, ok)
    for k, q in enumerate(peers):
        launch(True, lambda k=k, q=q: remote(
            meta.at[d], meta.at[d], md_send.at[k], md_recv.at[d], (q, z, c)))

    mine = z.astype(F32)

    def place(q):
        _, weight_q = selection(
            meta[q].reshape(n_z * tok, meta.shape[-1]), mine, capacity, padded, tok
        )
        weighted[q] = jnp.dot(weight_q, hid[q], preferred_element_type=F32).astype(BF)

    acc[...] = jnp.zeros_like(acc)
    dacc[...] = jnp.zeros_like(dacc)
    by_token = (((0,), (0,)), ((), ()))
    by_width = (((1,), (1,)), ((), ()))

    def back(jj):
        info = meta[d].reshape(n_z * tok, meta.shape[-1])
        pick, _ = selection(info, mine, capacity, padded, tok)

        def unit_of(i, _):
            j = jj + half * i
            for copy in weight_copies(j):
                copy.wait()
            tokens = rows[j].reshape(n_z * tok, unit)
            routed = lax.dot_general(pick, tokens, by_token, preferred_element_type=F32).astype(BF)
            acc[...] += lax.dot_general(routed, w[j], by_width, preferred_element_type=F32)
            dacc[...] += lax.dot_general(tokens, dw[j], by_width, preferred_element_type=F32)
            return 0

        lax.fori_loop(0, n_dp // half, unit_of, 0)

    def from_sibling(jj):
        j = (1 - c) * half + jj
        for dist in range(1, n_z):
            for zb, ok in ring(dist):
                pl.when(ok)(lambda: arrived(rows.at[j, zb], z_recv.at[j, zb]).wait_recv())

    for jj in range(half):
        for dist in range(1, n_z):
            if jj == half - 1 and dist == n_z - 2:
                pass_hidden()
            if jj == half - 1 and dist == n_z - 1:
                relay_slices(0)
                for q in peers:
                    arrived(meta.at[q], md_recv.at[q]).wait_recv()
                place(d)
                place(flip_x)
                place(flip_y)
                for copy in local_copies():
                    copy.wait()
                for early in range(half - 1):
                    from_sibling(early)
                    back(early)
            relay_rows(jj, dist)
            if dist == 1 and jj < half - 1:
                along_z(z, jj + 1, grad.at[:, cols(c * half + jj + 1)], yes)
    from_sibling(half - 1)
    own = pltpu.make_async_copy(rows.at[d], slices.at[d], loc.at[0])
    own.start()
    back(half - 1)

    _, weight = selection(meta[d].reshape(n_z * tok, meta.shape[-1]), mine, capacity, padded, tok)
    prob = lax.dot_general(
        weight, jnp.ones((n_z * tok, 128), BF), by_token, preferred_element_type=F32
    )[:slots, 0:1]
    back_hidden = acc[pl.ds(0, slots), :]
    up_val = up_pre[0].astype(F32)
    activated, slope = silu_parts(gate_pre[0].astype(F32))
    partial = jnp.sum(back_hidden * (activated * up_val), axis=1, keepdims=True)
    dots[0] = jnp.zeros(dots.shape[1:], F32)
    dots[0, pl.ds(0, slots), :] = jnp.broadcast_to(partial, (slots, 128))
    launch(True, lambda: remote(dots.at[0], dots.at[1], dot_send, dot_recv, sib))
    scaled = prob * back_hidden
    gate_out[0] = (scaled * up_val * slope).astype(BF)
    up_out[0] = (scaled * activated).astype(BF)
    dense_up = dense_up_pre[...].astype(F32)
    activated, slope = silu_parts(dense_gate_pre[...].astype(F32))
    dgate_out[...] = (dacc[...] * dense_up * slope).astype(BF)
    dup_out[...] = (dacc[...] * activated).astype(BF)

    for k in range(2):
        part = pl.ds(k * (padded // 2), padded // 2)
        dpart = pl.ds(k * (dh.shape[1] // 2), dh.shape[1] // 2)
        arrived(hid.at[diag, part], hf_recv.at[k]).wait_recv()
        arrived(dh.at[diag, dpart], df_recv.at[k]).wait_recv()
    place(diag)
    for dist in range(1, n_z):
        relay_slices(dist)
    arrived(dots.at[1], dot_recv).wait_recv()
    dots_out[...] = (dots[0] + dots[1]).T[0:1, :slots]
    own.wait()
    for cond, make in pending:
        when(cond, lambda: make().wait_send())


def layer(
    grad_out, ids, places, probs, expert_down, dense_down, gate_pre, up_pre, dense_gate, dense_up, n_dp, n_z
):
    tok, width = grad_out.shape
    unit = width // n_dp
    half = n_dp // 2
    _, slots, he = gate_pre.shape
    tokens, hd = dense_gate.shape
    padded = -(-slots // 32) * 32
    square = -(-slots // 128) * 128
    vm = pl.BlockSpec(memory_space=pltpu.VMEM)
    hbm = pl.BlockSpec(memory_space=pl.ANY)
    dma = pltpu.SemaphoreType.DMA
    shape = jax.ShapeDtypeStruct
    return pl.pallas_call(
        functools.partial(layer_kernel, n_dp, n_z),
        out_shape=(
            shape((n_dp, n_z, tok, unit), BF),
            shape((n_dp, tokens, he), BF),
            shape((n_dp, tokens, hd), BF),
            shape(gate_pre.shape, BF),
            shape(gate_pre.shape, BF),
            shape(dense_gate.shape, BF),
            shape(dense_gate.shape, BF),
            shape((1, slots), F32),
        ),
        in_specs=[hbm, vm, vm, vm, hbm, hbm, vm, vm, vm, vm],
        out_specs=(vm,) * 8,
        scratch_shapes=[
            pltpu.VMEM((n_dp, n_z, tok, unit), BF),
            pltpu.VMEM((n_dp, padded, he), BF),
            pltpu.VMEM((n_dp, n_z, tok, 128), BF),
            pltpu.VMEM((128, 128), F32),
            pltpu.VMEM((n_dp, he, unit), BF),
            pltpu.VMEM((n_dp, hd, unit), BF),
            pltpu.VMEM((padded, he), F32),
            pltpu.VMEM((tokens, hd), F32),
            pltpu.VMEM((2, square, 128), F32),
            dma((n_dp + 1,)), dma((n_dp,)), dma((n_dp,)),
            dma((2, half, n_z)), dma((n_dp, n_z)), dma((half, n_z)),
            dma((half, n_z)), dma((n_dp, n_z)), dma((n_dp, n_z)),
            dma((2, n_z)), dma((n_z,)), dma((n_dp,)), dma((n_dp,)),
            dma((2,)), dma((n_dp,)), dma((2,)), dma((n_dp,)),
            dma((2,)), dma((2,)), dma((2,)), dma((2,)), dma, dma, dma((2, n_dp)),
        ],
        compiler_params=pltpu.CompilerParams(
            collective_id=0, has_side_effects=True, vmem_limit_bytes=VMEM_LIMIT
        ),
    )(grad_out, ids, places, probs, expert_down, dense_down, gate_pre, up_pre, dense_gate, dense_up)


def final_kernel(scale, slices, weighted, dh, *refs):
    count = (len(refs) - 3) // 2
    given, (expert_out, dense_out), taken, sem = (
        refs[:count], refs[count:count + 2], refs[count + 2:-1], refs[-1]
    )
    copies = [pltpu.make_async_copy(a, b, sem.at[i]) for i, (a, b) in enumerate(zip(given, taken))]
    step = pl.program_id(0)

    @pl.when(step == 0)
    def _():
        for copy in copies:
            copy.start()

    contract = (((0,), (0,)), ((), ()))
    right = slices[...]
    expert_out[0] = (
        lax.dot_general(weighted[...], right, contract, preferred_element_type=F32) * scale
    ).astype(BF)
    dense_out[...] = (
        lax.dot_general(dh[...], right, contract, preferred_element_type=F32) * scale
    ).astype(BF)

    @pl.when(step == pl.num_programs(0) - 1)
    def _():
        for copy in copies:
            copy.wait()


def final(slices, weighted, dh, small, scale):
    tokens, unit = slices.shape
    he, hd = weighted.shape[1], dh.shape[1]
    tile = unit // 2 if unit % 256 == 0 else unit
    hbm = pl.BlockSpec(memory_space=pl.ANY)
    shape = jax.ShapeDtypeStruct
    return pl.pallas_call(
        functools.partial(final_kernel, scale),
        grid=(unit // tile,),
        out_shape=(shape((1, he, unit), BF), shape((hd, unit), BF))
        + tuple(shape(a.shape, a.dtype) for a in small),
        in_specs=[
            pl.BlockSpec((tokens, tile), lambda i: (0, i)),
            pl.BlockSpec((tokens, he), lambda i: (0, 0)),
            pl.BlockSpec((tokens, hd), lambda i: (0, 0)),
        ] + [hbm] * len(small),
        out_specs=(
            pl.BlockSpec((1, he, tile), lambda i: (0, 0, i)),
            pl.BlockSpec((hd, tile), lambda i: (0, i)),
        ) + (hbm,) * len(small),
        scratch_shapes=[pltpu.SemaphoreType.DMA((len(small),))],
        compiler_params=pltpu.CompilerParams(vmem_limit_bytes=VMEM_LIMIT),
    )(slices, weighted, dh, *small)


def local_fast(
    grad_out, gate_prob, expert_ids, slot_positions, expert_down, dense_down,
    expert_gate_pre, expert_up_pre, dense_gate_pre, dense_up_pre,
):
    n_z = lax.axis_size("expert")
    n_dp = lax.axis_size("dp")
    slices, weighted, dh, *small = layer(
        grad_out, expert_ids.T, slot_positions.T, gate_prob.T, expert_down, dense_down,
        expert_gate_pre, expert_up_pre, dense_gate_pre, dense_up_pre, n_dp, n_z,
    )
    tokens = slices.shape[0] * slices.shape[1] * slices.shape[2]
    expert_grad, dense_grad, gate_grad, up_grad, dgate_grad, dup_grad, dots = final(
        slices.reshape(tokens, -1), weighted.reshape(tokens, -1), dh.reshape(tokens, -1), small, 1.0 / n_dp
    )
    return (gate_grad, up_grad, dots, expert_grad.transpose(0, 2, 1), dgate_grad, dup_grad, dense_grad.T)


def local_plain(
    grad_out,
    gate_prob,
    expert_ids,
    slot_positions,
    expert_down,
    dense_down,
    expert_gate_pre,
    expert_up_pre,
    dense_gate_pre,
    dense_up_pre,
):
    n_expert = lax.axis_size("expert")
    n_replica = lax.axis_size("dp")
    width = grad_out.shape[1]
    capacity = expert_gate_pre.shape[1] // n_expert
    flat_ids = expert_ids.reshape(-1)
    flat_slots = slot_positions.reshape(-1)
    repeated = jnp.repeat(grad_out, 2, axis=0)
    send_rows = (
        jnp.zeros((n_expert, capacity, width), jnp.bfloat16).at[flat_ids, flat_slots].set(repeated)
    )
    send_prob = (
        jnp.zeros((n_expert, capacity), jnp.bfloat16)
        .at[flat_ids, flat_slots]
        .set(gate_prob.reshape(-1))
    )
    recv_rows, recv_prob = (
        lax.all_to_all(send_rows, "expert", split_axis=0, concat_axis=0, tiled=True),
        lax.all_to_all(send_prob, "expert", split_axis=0, concat_axis=0, tiled=True),
    )
    slot_rows = recv_rows.reshape(n_expert * capacity, width)
    slot_prob = recv_prob.reshape(-1).astype(jnp.float32)
    weight_local = expert_down[0]
    back_hidden = lax.dot_general(
        slot_rows, weight_local, (((1,), (1,)), ((), ())), preferred_element_type=jnp.float32
    )
    gate_val = expert_gate_pre[0].astype(jnp.float32)
    up_val = expert_up_pre[0].astype(jnp.float32)
    activated, slope = silu_parts(gate_val)
    hidden = activated * up_val
    partial_dots = jnp.sum(back_hidden * hidden, axis=1)
    slot_dots = lax.psum(partial_dots, "tensor")
    scaled = slot_prob[:, None] * back_hidden
    expert_gate_grad = (scaled * up_val * slope).astype(jnp.bfloat16)[None]
    expert_up_grad = (scaled * activated).astype(jnp.bfloat16)[None]
    weighted = (slot_prob[:, None] * hidden).astype(jnp.bfloat16)
    expert_summed = lax.psum_scatter(
        lax.dot_general(
            slot_rows, weighted, (((0,), (0,)), ((), ())), preferred_element_type=jnp.float32
        ).astype(jnp.bfloat16),
        "dp",
        scatter_dimension=0,
        tiled=True,
    ).astype(jnp.float32)
    expert_down_grad = (expert_summed / n_replica).astype(jnp.bfloat16)[None]
    shard_rows = lax.all_gather(grad_out, "expert", axis=0, tiled=True)
    back_dense = lax.dot_general(
        shard_rows, dense_down, (((1,), (1,)), ((), ())), preferred_element_type=jnp.float32
    )
    dense_gate = dense_gate_pre.astype(jnp.float32)
    dense_up = dense_up_pre.astype(jnp.float32)
    dense_act, dense_slope = silu_parts(dense_gate)
    gate_buffer = (back_dense * dense_up * dense_slope).astype(jnp.bfloat16)
    up_buffer = (back_dense * dense_act).astype(jnp.bfloat16)
    dense_hidden = (dense_act * dense_up).astype(jnp.bfloat16)
    weight_sum = lax.dot_general(
        shard_rows, dense_hidden, (((0,), (0,)), ((), ())), preferred_element_type=jnp.float32
    )
    dense_summed = lax.psum_scatter(
        weight_sum.astype(jnp.bfloat16), "dp", scatter_dimension=0, tiled=True
    ).astype(jnp.float32)
    dense_down_grad = (dense_summed / n_replica).astype(jnp.bfloat16)
    return (
        expert_gate_grad,
        expert_up_grad,
        slot_dots[None],
        expert_down_grad,
        gate_buffer,
        up_buffer,
        dense_down_grad,
    )


def solution(mesh):
    sizes = mesh.shape
    fits = sizes["tensor"] == 2 and sizes["dp"] == 4

    def local(*args):
        aligned = args[0].shape[1] % (sizes["dp"] * 128) == 0 and args[0].shape[0] % 16 == 0
        return (local_fast if fits and aligned else local_plain)(*args)

    return jax.shard_map(
        local,
        mesh=mesh,
        in_specs=(
            P(("dp", "expert"), None),
            P(("dp", "expert"), None),
            P(("dp", "expert"), None),
            P(("dp", "expert"), None),
            P("expert", "tensor", None),
            P(("expert", "tensor"), None),
            P("expert", "dp", "tensor"),
            P("expert", "dp", "tensor"),
            P("dp", ("expert", "tensor")),
            P("dp", ("expert", "tensor")),
        ),
        out_specs=(
            P("expert", "dp", "tensor"),
            P("expert", "dp", "tensor"),
            P("expert", "dp"),
            P("expert", "dp", "tensor"),
            P("dp", ("expert", "tensor")),
            P("dp", ("expert", "tensor")),
            P("dp", ("expert", "tensor")),
        ),
        check_vma=False,
    )
```

```python
import functools

import jax
import jax.numpy as jnp
from jax import lax
from jax.experimental import pallas as pl
from jax.experimental.pallas import tpu as pltpu
from jax.sharding import PartitionSpec as P

MESH = pl.DeviceIdType.MESH
BF = jnp.bfloat16
F32 = jnp.float32
VMEM_LIMIT = 60 * 2**20


def silu_parts(gate_val):
    gate_sig = jax.nn.sigmoid(gate_val)
    activated = gate_val * gate_sig
    slope = gate_sig * (1.0 + gate_val * (1.0 - gate_sig))
    return (activated, slope)


def selection(info, mine, capacity, slots, tok):
    info = info.astype(F32)
    tokens = info.shape[0]
    block = lax.broadcasted_iota(jnp.int32, (tokens, slots), 0) // tok
    span = (lax.broadcasted_iota(jnp.int32, (tokens, slots), 1) - block * capacity).astype(F32)
    first = (info[:, 0:1] == mine) & (info[:, 2:3] == span)
    second = (info[:, 1:2] == mine) & (info[:, 3:4] == span)
    weight = jnp.where(first, info[:, 4:5], 0.0) + jnp.where(second, info[:, 5:6], 0.0)
    pick = jnp.where(first | second, 1.0, 0.0)
    return pick.astype(BF), weight.astype(BF)


def layer_kernel(
    n_dp, n_z, grad, ids, places, probs, expert_w, dense_w, gate_pre, up_pre, dense_gate_pre, dense_up_pre,
    slices, weighted, dh, gate_out, up_out, dgate_out, dup_out, dots_out,
    rows, hid, meta, table, w, dw, acc, dacc, dots,
    loc, w_sem, dw_sem, z_send, z_recv, sib_send, sl_send, sl_recv, slf_send,
    mz_send, mz_recv, md_send, md_recv, hid_send, hid_recv, dh_send, dh_recv,
    hf_send, hf_recv, df_send, df_recv, dot_send, dot_recv, slz_send,
):
    d, z, c = lax.axis_index("dp"), lax.axis_index("expert"), lax.axis_index("tensor")
    half = n_dp // 2
    tok = grad.shape[0]
    unit = grad.shape[1] // n_dp
    slots = gate_pre.shape[1]
    padded = hid.shape[1]
    capacity = slots // n_z
    sib = (d, z, 1 - c)
    flip_x = d + 1 - 2 * lax.rem(d, 2)
    flip_y = lax.rem(d + 2, n_dp)
    diag = lax.rem(flip_x + 2, n_dp)
    peers = [flip_x, flip_y, diag]

    def remote(src, dst, ssem, rsem, dev):
        return pltpu.make_async_remote_copy(
            src_ref=src, dst_ref=dst, send_sem=ssem, recv_sem=rsem, device_id=dev, device_id_type=MESH
        )

    def when(cond, fn):
        if cond is True:
            fn()
        else:
            pl.when(cond)(fn)

    pending = []

    def launch(cond, make):
        when(cond, lambda: make().start())
        pending.append((cond, make))

    barrier = pltpu.get_barrier_semaphore()

    def greet(dev):
        pl.semaphore_signal(barrier, inc=1, device_id=dev, device_id_type=MESH)

    greet(sib)
    for q in peers:
        greet((q, z, c))
    pl.when(z > 0)(lambda: greet((d, z - 1, c)))
    pl.when(z < n_z - 1)(lambda: greet((d, z + 1, c)))

    def cols(j):
        return pl.ds(pl.multiple_of(j * unit, unit), unit)

    def local_copies():
        return [
            pltpu.make_async_copy(grad.at[:, pl.ds(j * unit, unit)], rows.at[j, z], loc.at[j])
            for j in range(n_dp)
        ]

    def weight_copies(j):
        return (
            pltpu.make_async_copy(expert_w.at[0, :, cols(j)], w.at[j], w_sem.at[j]),
            pltpu.make_async_copy(dense_w.at[:, cols(j)], dw.at[j], dw_sem.at[j]),
        )

    for copy in local_copies():
        copy.start()
    table[...] = jnp.zeros(table.shape, F32)
    for k, ref in enumerate((ids, places, probs)):
        table[pl.ds(2 * k, 2), pl.ds(0, tok)] = ref[...].astype(F32)
    meta[d, z] = table[...].T[:tok].astype(BF)
    pl.semaphore_wait(barrier, n_dp + jnp.where(z > 0, 1, 0) + jnp.where(z < n_z - 1, 1, 0))

    def along_z(zb, jj, src, ok):
        j = c * half + jj
        launch(ok & (zb <= z) & (z < n_z - 1), lambda: remote(
            src, rows.at[j, zb], z_send.at[0, jj, zb], z_recv.at[j, zb], (d, z + 1, c)))
        launch(ok & (zb >= z) & (z > 0), lambda: remote(
            src, rows.at[j, zb], z_send.at[1, jj, zb], z_recv.at[j, zb], (d, z - 1, c)))

    def over_dp(zb, jj, src, ok):
        j = c * half + jj
        launch(ok & (j != d), lambda: remote(
            src, slices.at[d, zb], sl_send.at[jj, zb], sl_recv.at[d, zb], (j, z, c)))

    def spread_meta(zb, ok):
        src = meta.at[d, zb]
        launch(ok & (zb <= z) & (z < n_z - 1), lambda: remote(
            src, src, mz_send.at[0, zb], mz_recv.at[zb], (d, z + 1, c)))
        launch(ok & (zb >= z) & (z > 0), lambda: remote(
            src, src, mz_send.at[1, zb], mz_recv.at[zb], (d, z - 1, c)))

    yes = z >= 0
    spread_meta(z, yes)
    along_z(z, 0, grad.at[:, cols(c * half)], yes)
    for jj in range(half):
        over_dp(z, jj, grad.at[:, cols(c * half + jj)], yes)

    hid[d] = jnp.zeros(hid.shape[1:], BF)
    activated, _ = silu_parts(gate_pre[0].astype(F32))
    hid[d, pl.ds(0, slots), :] = (activated * up_pre[0].astype(F32)).astype(BF)
    activated, _ = silu_parts(dense_gate_pre[...].astype(F32))
    dh[d] = (activated * dense_up_pre[...].astype(F32)).astype(BF)
    for k, q in enumerate(peers[:2]):
        launch(True, lambda k=k, q=q: remote(
            hid.at[d], hid.at[d], hid_send.at[k], hid_recv.at[d], (q, z, c)))
        launch(True, lambda k=k, q=q: remote(
            dh.at[d], dh.at[d], dh_send.at[k], dh_recv.at[d], (q, z, c)))

    def arrived(dst, rsem):
        return remote(dst, dst, loc.at[0], rsem, sib)

    def pass_hidden():
        for k, (source, target) in enumerate(((flip_x, flip_y), (flip_y, flip_x))):
            arrived(hid.at[source], hid_recv.at[source]).wait_recv()
            arrived(dh.at[source], dh_recv.at[source]).wait_recv()
            part = pl.ds(k * (padded // 2), padded // 2)
            dpart = pl.ds(k * (dh.shape[1] // 2), dh.shape[1] // 2)
            launch(True, lambda k=k, source=source, target=target, part=part: remote(
                hid.at[source, part], hid.at[source, part], hf_send.at[k], hf_recv.at[k], (target, z, c)))
            launch(True, lambda k=k, source=source, target=target, dpart=dpart: remote(
                dh.at[source, dpart], dh.at[source, dpart], df_send.at[k], df_recv.at[k], (target, z, c)))

    own_half = c == d // half

    def pass_slices(zb, ok, own=False):
        for q in peers:
            pl.when(ok)(lambda: arrived(slices.at[q, zb], sl_recv.at[q, zb]).wait_recv())
            launch(ok & own_half, lambda q=q: remote(
                slices.at[q, zb], slices.at[q, zb], slf_send.at[q, zb], sl_recv.at[q, zb], sib))
            for k, (step, there) in enumerate(((1, z < n_z - 1), (-1, z > 0)) if own else ()):
                launch(own_half & there, lambda q=q, k=k, step=step: remote(
                    slices.at[q, zb], slices.at[q, zb], slz_send.at[k, q], sl_recv.at[q, zb],
                    (d, z + step, c)))

    def fetch_weights(jj):
        for i in range(n_dp // half):
            for copy in weight_copies(jj + half * i):
                copy.start()

    fetch_weights(0)

    def ring(dist):
        return [(zb, (zb >= 0) & (zb < n_z)) for zb in (z - dist, z + dist)]

    def relay_rows(jj, dist):
        j = c * half + jj
        for zb, ok in ring(dist):
            pl.when(ok)(lambda: arrived(rows.at[j, zb], z_recv.at[j, zb]).wait_recv())
            along_z(zb, jj, rows.at[j, zb], ok)
            launch(ok, lambda zb=zb: remote(
                rows.at[j, zb], rows.at[j, zb], sib_send.at[jj, zb], z_recv.at[j, zb], sib))
            if dist > 1:
                over_dp(zb, jj, rows.at[j, zb], ok)

    def relay_slices(dist):
        for zb, ok in [(z, yes)] if dist == 0 else ring(dist):
            pass_slices(zb, ok, dist == 0)

    for dist in range(1, n_z):
        for zb, ok in ring(dist):
            pl.when(ok)(lambda: arrived(meta.at[d, zb], mz_recv.at[zb]).wait_recv())
            spread_meta(zb, ok)
    for k, q in enumerate(peers):
        launch(True, lambda k=k, q=q: remote(
            meta.at[d], meta.at[d], md_send.at[k], md_recv.at[d], (q, z, c)))

    mine = z.astype(F32)

    def place(q):
        _, weight_q = selection(
            meta[q].reshape(n_z * tok, meta.shape[-1]), mine, capacity, padded, tok
        )
        weighted[q] = jnp.dot(weight_q, hid[q], preferred_element_type=F32).astype(BF)

    acc[...] = jnp.zeros_like(acc)
    dacc[...] = jnp.zeros_like(dacc)
    by_token = (((0,), (0,)), ((), ()))
    by_width = (((1,), (1,)), ((), ()))

    def back(jj):
        info = meta[d].reshape(n_z * tok, meta.shape[-1])
        pick, _ = selection(info, mine, capacity, padded, tok)

        def unit_of(i, _):
            j = jj + half * i
            for copy in weight_copies(j):
                copy.wait()
            tokens = rows[j].reshape(n_z * tok, unit)
            routed = lax.dot_general(pick, tokens, by_token, preferred_element_type=F32).astype(BF)
            acc[...] += lax.dot_general(routed, w[j], by_width, preferred_element_type=F32)
            dacc[...] += lax.dot_general(tokens, dw[j], by_width, preferred_element_type=F32)
            return 0

        lax.fori_loop(0, n_dp // half, unit_of, 0)

    def from_sibling(jj):
        j = (1 - c) * half + jj
        for dist in range(1, n_z):
            for zb, ok in ring(dist):
                pl.when(ok)(lambda: arrived(rows.at[j, zb], z_recv.at[j, zb]).wait_recv())

    for jj in range(half):
        for dist in range(1, n_z):
            if jj == half - 1 and dist == n_z - 2:
                pass_hidden()
            if jj == half - 1 and dist == n_z - 1:
                relay_slices(0)
                for q in peers:
                    arrived(meta.at[q], md_recv.at[q]).wait_recv()
                place(d)
                place(flip_x)
                place(flip_y)
                for copy in local_copies():
                    copy.wait()
                for early in range(half - 1):
                    from_sibling(early)
                    back(early)
            relay_rows(jj, dist)
            if dist == 2 and jj < half - 1:
                fetch_weights(jj + 1)
            if dist == 1 and jj < half - 1:
                along_z(z, jj + 1, grad.at[:, cols(c * half + jj + 1)], yes)
    from_sibling(half - 1)
    own = pltpu.make_async_copy(rows.at[d], slices.at[d], loc.at[0])
    own.start()
    back(half - 1)

    _, weight = selection(meta[d].reshape(n_z * tok, meta.shape[-1]), mine, capacity, padded, tok)
    prob = lax.dot_general(
        weight, jnp.ones((n_z * tok, 128), BF), by_token, preferred_element_type=F32
    )[:slots, 0:1]
    back_hidden = acc[pl.ds(0, slots), :]
    up_val = up_pre[0].astype(F32)
    activated, slope = silu_parts(gate_pre[0].astype(F32))
    partial = jnp.sum(back_hidden * (activated * up_val), axis=1, keepdims=True)
    dots[0] = jnp.zeros(dots.shape[1:], F32)
    dots[0, pl.ds(0, slots), :] = jnp.broadcast_to(partial, (slots, 128))
    launch(True, lambda: remote(dots.at[0], dots.at[1], dot_send, dot_recv, sib))
    scaled = prob * back_hidden
    gate_out[0] = (scaled * up_val * slope).astype(BF)
    up_out[0] = (scaled * activated).astype(BF)
    dense_up = dense_up_pre[...].astype(F32)
    activated, slope = silu_parts(dense_gate_pre[...].astype(F32))
    dgate_out[...] = (dacc[...] * dense_up * slope).astype(BF)
    dup_out[...] = (dacc[...] * activated).astype(BF)

    for k in range(2):
        part = pl.ds(k * (padded // 2), padded // 2)
        dpart = pl.ds(k * (dh.shape[1] // 2), dh.shape[1] // 2)
        arrived(hid.at[diag, part], hf_recv.at[k]).wait_recv()
        arrived(dh.at[diag, dpart], df_recv.at[k]).wait_recv()
    place(diag)
    for dist in range(1, n_z):
        relay_slices(dist)
    arrived(dots.at[1], dot_recv).wait_recv()
    dots_out[...] = (dots[0] + dots[1]).T[0:1, :slots]
    own.wait()
    for cond, make in pending:
        when(cond, lambda: make().wait_send())


def layer(
    grad_out, ids, places, probs, expert_down, dense_down, gate_pre, up_pre, dense_gate, dense_up, n_dp, n_z
):
    tok, width = grad_out.shape
    unit = width // n_dp
    half = n_dp // 2
    _, slots, he = gate_pre.shape
    tokens, hd = dense_gate.shape
    padded = -(-slots // 32) * 32
    square = -(-slots // 128) * 128
    vm = pl.BlockSpec(memory_space=pltpu.VMEM)
    hbm = pl.BlockSpec(memory_space=pl.ANY)
    dma = pltpu.SemaphoreType.DMA
    shape = jax.ShapeDtypeStruct
    return pl.pallas_call(
        functools.partial(layer_kernel, n_dp, n_z),
        out_shape=(
            shape((n_dp, n_z, tok, unit), BF),
            shape((n_dp, tokens, he), BF),
            shape((n_dp, tokens, hd), BF),
            shape(gate_pre.shape, BF),
            shape(gate_pre.shape, BF),
            shape(dense_gate.shape, BF),
            shape(dense_gate.shape, BF),
            shape((1, slots), F32),
        ),
        in_specs=[hbm, vm, vm, vm, hbm, hbm, vm, vm, vm, vm],
        out_specs=(vm,) * 8,
        scratch_shapes=[
            pltpu.VMEM((n_dp, n_z, tok, unit), BF),
            pltpu.VMEM((n_dp, padded, he), BF),
            pltpu.VMEM((n_dp, n_z, tok, 128), BF),
            pltpu.VMEM((128, 128), F32),
            pltpu.VMEM((n_dp, he, unit), BF),
            pltpu.VMEM((n_dp, hd, unit), BF),
            pltpu.VMEM((padded, he), F32),
            pltpu.VMEM((tokens, hd), F32),
            pltpu.VMEM((2, square, 128), F32),
            dma((n_dp + 1,)), dma((n_dp,)), dma((n_dp,)),
            dma((2, half, n_z)), dma((n_dp, n_z)), dma((half, n_z)),
            dma((half, n_z)), dma((n_dp, n_z)), dma((n_dp, n_z)),
            dma((2, n_z)), dma((n_z,)), dma((n_dp,)), dma((n_dp,)),
            dma((2,)), dma((n_dp,)), dma((2,)), dma((n_dp,)),
            dma((2,)), dma((2,)), dma((2,)), dma((2,)), dma, dma, dma((2, n_dp)),
        ],
        compiler_params=pltpu.CompilerParams(
            collective_id=0, has_side_effects=True, vmem_limit_bytes=VMEM_LIMIT
        ),
    )(grad_out, ids, places, probs, expert_down, dense_down, gate_pre, up_pre, dense_gate, dense_up)


def final_kernel(scale, slices, weighted, dh, *refs):
    count = (len(refs) - 2) // 2
    given, (expert_out, dense_out), taken = refs[:count], refs[count:count + 2], refs[count + 2:]

    @pl.when(pl.program_id(0) == 0)
    def _():
        for a, b in zip(given, taken):
            b[...] = a[...]

    contract = (((0,), (0,)), ((), ()))
    right = slices[...]
    expert_out[0] = (
        lax.dot_general(weighted[...], right, contract, preferred_element_type=F32) * scale
    ).astype(BF)
    dense_out[...] = (
        lax.dot_general(dh[...], right, contract, preferred_element_type=F32) * scale
    ).astype(BF)


def final(slices, weighted, dh, small, scale):
    tokens, unit = slices.shape
    he, hd = weighted.shape[1], dh.shape[1]
    tile = unit // 2 if unit % 256 == 0 else unit
    shape = jax.ShapeDtypeStruct
    whole = [pl.BlockSpec(a.shape, lambda i, n=a.ndim: (0,) * n) for a in small]
    return pl.pallas_call(
        functools.partial(final_kernel, scale),
        grid=(unit // tile,),
        out_shape=(shape((1, he, unit), BF), shape((hd, unit), BF))
        + tuple(shape(a.shape, a.dtype) for a in small),
        in_specs=[
            pl.BlockSpec((tokens, tile), lambda i: (0, i)),
            pl.BlockSpec((tokens, he), lambda i: (0, 0)),
            pl.BlockSpec((tokens, hd), lambda i: (0, 0)),
        ] + whole,
        out_specs=(
            pl.BlockSpec((1, he, tile), lambda i: (0, 0, i)),
            pl.BlockSpec((hd, tile), lambda i: (0, i)),
        ) + tuple(whole),
        compiler_params=pltpu.CompilerParams(vmem_limit_bytes=VMEM_LIMIT),
    )(slices, weighted, dh, *small)


def local_fast(
    grad_out, gate_prob, expert_ids, slot_positions, expert_down, dense_down,
    expert_gate_pre, expert_up_pre, dense_gate_pre, dense_up_pre,
):
    n_z = lax.axis_size("expert")
    n_dp = lax.axis_size("dp")
    slices, weighted, dh, *small = layer(
        grad_out, expert_ids.T, slot_positions.T, gate_prob.T, expert_down, dense_down,
        expert_gate_pre, expert_up_pre, dense_gate_pre, dense_up_pre, n_dp, n_z,
    )
    tokens = slices.shape[0] * slices.shape[1] * slices.shape[2]
    expert_grad, dense_grad, gate_grad, up_grad, dgate_grad, dup_grad, dots = final(
        slices.reshape(tokens, -1), weighted.reshape(tokens, -1), dh.reshape(tokens, -1), small, 1.0 / n_dp
    )
    return (gate_grad, up_grad, dots, expert_grad.transpose(0, 2, 1), dgate_grad, dup_grad, dense_grad.T)


def local_plain(
    grad_out,
    gate_prob,
    expert_ids,
    slot_positions,
    expert_down,
    dense_down,
    expert_gate_pre,
    expert_up_pre,
    dense_gate_pre,
    dense_up_pre,
):
    n_expert = lax.axis_size("expert")
    n_replica = lax.axis_size("dp")
    width = grad_out.shape[1]
    capacity = expert_gate_pre.shape[1] // n_expert
    flat_ids = expert_ids.reshape(-1)
    flat_slots = slot_positions.reshape(-1)
    repeated = jnp.repeat(grad_out, 2, axis=0)
    send_rows = (
        jnp.zeros((n_expert, capacity, width), jnp.bfloat16).at[flat_ids, flat_slots].set(repeated)
    )
    send_prob = (
        jnp.zeros((n_expert, capacity), jnp.bfloat16)
        .at[flat_ids, flat_slots]
        .set(gate_prob.reshape(-1))
    )
    recv_rows, recv_prob = (
        lax.all_to_all(send_rows, "expert", split_axis=0, concat_axis=0, tiled=True),
        lax.all_to_all(send_prob, "expert", split_axis=0, concat_axis=0, tiled=True),
    )
    slot_rows = recv_rows.reshape(n_expert * capacity, width)
    slot_prob = recv_prob.reshape(-1).astype(jnp.float32)
    weight_local = expert_down[0]
    back_hidden = lax.dot_general(
        slot_rows, weight_local, (((1,), (1,)), ((), ())), preferred_element_type=jnp.float32
    )
    gate_val = expert_gate_pre[0].astype(jnp.float32)
    up_val = expert_up_pre[0].astype(jnp.float32)
    activated, slope = silu_parts(gate_val)
    hidden = activated * up_val
    partial_dots = jnp.sum(back_hidden * hidden, axis=1)
    slot_dots = lax.psum(partial_dots, "tensor")
    scaled = slot_prob[:, None] * back_hidden
    expert_gate_grad = (scaled * up_val * slope).astype(jnp.bfloat16)[None]
    expert_up_grad = (scaled * activated).astype(jnp.bfloat16)[None]
    weighted = (slot_prob[:, None] * hidden).astype(jnp.bfloat16)
    expert_summed = lax.psum_scatter(
        lax.dot_general(
            slot_rows, weighted, (((0,), (0,)), ((), ())), preferred_element_type=jnp.float32
        ).astype(jnp.bfloat16),
        "dp",
        scatter_dimension=0,
        tiled=True,
    ).astype(jnp.float32)
    expert_down_grad = (expert_summed / n_replica).astype(jnp.bfloat16)[None]
    shard_rows = lax.all_gather(grad_out, "expert", axis=0, tiled=True)
    back_dense = lax.dot_general(
        shard_rows, dense_down, (((1,), (1,)), ((), ())), preferred_element_type=jnp.float32
    )
    dense_gate = dense_gate_pre.astype(jnp.float32)
    dense_up = dense_up_pre.astype(jnp.float32)
    dense_act, dense_slope = silu_parts(dense_gate)
    gate_buffer = (back_dense * dense_up * dense_slope).astype(jnp.bfloat16)
    up_buffer = (back_dense * dense_act).astype(jnp.bfloat16)
    dense_hidden = (dense_act * dense_up).astype(jnp.bfloat16)
    weight_sum = lax.dot_general(
        shard_rows, dense_hidden, (((0,), (0,)), ((), ())), preferred_element_type=jnp.float32
    )
    dense_summed = lax.psum_scatter(
        weight_sum.astype(jnp.bfloat16), "dp", scatter_dimension=0, tiled=True
    ).astype(jnp.float32)
    dense_down_grad = (dense_summed / n_replica).astype(jnp.bfloat16)
    return (
        expert_gate_grad,
        expert_up_grad,
        slot_dots[None],
        expert_down_grad,
        gate_buffer,
        up_buffer,
        dense_down_grad,
    )


def solution(mesh):
    sizes = mesh.shape
    fits = sizes["tensor"] == 2 and sizes["dp"] == 4

    def local(*args):
        aligned = args[0].shape[1] % (sizes["dp"] * 128) == 0 and args[0].shape[0] % 16 == 0
        return (local_fast if fits and aligned else local_plain)(*args)

    return jax.shard_map(
        local,
        mesh=mesh,
        in_specs=(
            P(("dp", "expert"), None),
            P(("dp", "expert"), None),
            P(("dp", "expert"), None),
            P(("dp", "expert"), None),
            P("expert", "tensor", None),
            P(("expert", "tensor"), None),
            P("expert", "dp", "tensor"),
            P("expert", "dp", "tensor"),
            P("dp", ("expert", "tensor")),
            P("dp", ("expert", "tensor")),
        ),
        out_specs=(
            P("expert", "dp", "tensor"),
            P("expert", "dp", "tensor"),
            P("expert", "dp"),
            P("expert", "dp", "tensor"),
            P("dp", ("expert", "tensor")),
            P("dp", ("expert", "tensor")),
            P("dp", ("expert", "tensor")),
        ),
        check_vma=False,
    )
```
